32 devices in a mesh: gz: 4 (over z), gy: 2 (over y), gx: 4 (over x, core).
Axes of the slice: x: 2, y: 2, z: 4, core: 2. Of those that a mesh axis runs over, the one named last changes fastest.
Arguments:
- ref_image: float32 [64, 128, 512], P('gz', 'gy', 'gx'), may hold values from -40 to 40
- deformed_image: float32 [64, 128, 512], P('gz', 'gy', 'gx'), may hold values from -40 to 40
- nodal_disp: int32 [3, 8, 10, 36], P(None, 'gz', 'gy', 'gx'), may hold values from -1024 to 1023, as said below
Outputs:
- update: float32 [3, 8, 10, 36], P(None, 'gz', 'gy', 'gx')
- cg_residual: float32 [3, 8, 10, 36], P(None, 'gz', 'gy', 'gx')
The draws below stay inside these ranges and needn't reach their ends.
Inputs may be any that keep to these rules, and one draw needn't show every extreme that they name: `nodal_disp`: copies of a node held by neighbouring bricks are equal.
All inputs are finite; a program needn't handle non-finite values.
Results may differ from the reference program's by a relative error of at most 0.0003.
Values sent between devices are 32-bit elements; how exact they have to be, the bound alone decides.
A program may use at most 256 MiB of HBM per device.

```python
import jax
import jax.numpy as jnp
import numpy as np
from jax import lax

ELEM = 16
EZ = 1
EY = 4
EX = 8
CGSTEPS = 8
NZ = 64
NY = 128
NX = 512
N_GZ = 4
N_GY = 2
N_GX = 4


def contrast():
    depth = jnp.arange(NZ, dtype=jnp.float32) / NZ
    across = jnp.arange(NY, dtype=jnp.float32) / NY
    along = jnp.arange(NX, dtype=jnp.float32) / NX
    return 10.0 ** ((depth[:, None, None] + across[None, :, None] + along[None, None, :]) / 3.0)


def draw_ref_image(key, part):
    key = jax.random.fold_in(key, 11)
    noise = jnp.clip(jax.random.normal(key, (NZ, NY, NX), jnp.float32), -3.5, 3.5)
    return contrast() * noise


def draw_deformed_image(key, part):
    key = jax.random.fold_in(key, 13)
    noise = jnp.clip(jax.random.normal(key, (NZ, NY, NX), jnp.float32), -3.5, 3.5)
    return contrast() * noise


def draw_nodal_disp(key, part):
    key = jax.random.fold_in(key, 17)
    first_key, second_key, third_key = jax.random.split(key, 3)
    nodes_z = EZ * N_GZ + 1
    nodes_y = EY * N_GY + 1
    nodes_x = EX * N_GX + 1
    field = jax.random.randint(first_key, (3, nodes_z, nodes_y, nodes_x), -1024, 1024, dtype=jnp.int32)
    flat = field.reshape(-1)
    middle = flat.shape[0] // 2
    lowest = jax.random.randint(second_key, (), 0, middle, dtype=jnp.int32)
    highest = jax.random.randint(third_key, (), middle, flat.shape[0], dtype=jnp.int32)
    flat = flat.at[lowest].set(-1024).at[highest].set(1023)
    field = flat.reshape((3, nodes_z, nodes_y, nodes_x))
    for axis, (groups, elems) in enumerate(((N_GZ, EZ), (N_GY, EY), (N_GX, EX))):
        index = (np.arange(groups)[:, None] * elems + np.arange(elems + 1)[None, :]).ravel()
        field = jnp.take(field, jnp.asarray(index, dtype=jnp.int32), axis=axis + 1)
    return field


def setup_inputs(seed: int = 0) -> dict:
    key_of = jax.random.split(jax.random.key(seed), 4)
    return {
        "ref_image": draw_ref_image(jax.random.fold_in(key_of[3], 71), 0),
        "deformed_image": draw_deformed_image(jax.random.fold_in(key_of[3], 71), 0),
        "nodal_disp": draw_nodal_disp(jax.random.fold_in(key_of[3], 71), 0),
    }


quantum = 64
damping = 0.5


def weights():
    position = (jnp.arange(ELEM, dtype=jnp.float32) + 0.5) / ELEM
    return jnp.stack([1.0 - position, position])


def corners(field):
    count_z, count_y, count_x = field.shape[1] - 1, field.shape[2] - 1, field.shape[3] - 1
    pieces = []
    for offset in range(8):
        along_z, along_y, along_x = offset >> 2, (offset >> 1) & 1, offset & 1
        pieces.append(field[:, along_z:along_z + count_z, along_y:along_y + count_y, along_x:along_x + count_x])
    return jnp.stack(pieces, axis=1).reshape((field.shape[0], 2, 2, 2, count_z, count_y, count_x))


def assemble(parts):
    total = 0.0
    for offset in range(8):
        along_z, along_y, along_x = offset >> 2, (offset >> 1) & 1, offset & 1
        total = total + jnp.pad(parts[:, along_z, along_y, along_x], ((0, 0), (along_z, 1 - along_z), (along_y, 1 - along_y), (along_x, 1 - along_x)))
    return total


def blocks(volume):
    lead = volume.shape[:-3]
    count_z, count_y, count_x = volume.shape[-3] // ELEM, volume.shape[-2] // ELEM, volume.shape[-1] // ELEM
    shaped = volume.reshape(lead + (count_z, ELEM, count_y, ELEM, count_x, ELEM))
    number = len(lead)
    order = tuple(range(number)) + (number + 1, number + 3, number + 5, number, number + 2, number + 4)
    return jnp.transpose(shaped, order).reshape(lead + (ELEM, ELEM, ELEM, count_z * count_y * count_x))


def element_terms(ref_pad, deformed_pad, nodes):
    count_z, count_y, count_x = nodes.shape[1] - 1, nodes.shape[2] - 1, nodes.shape[3] - 1
    image = ref_pad[1:-1, 1:-1, 1:-1]
    gradient = jnp.stack([
        0.5 * (ref_pad[2:, 1:-1, 1:-1] - ref_pad[:-2, 1:-1, 1:-1]),
        0.5 * (ref_pad[1:-1, 2:, 1:-1] - ref_pad[1:-1, :-2, 1:-1]),
        0.5 * (ref_pad[1:-1, 1:-1, 2:] - ref_pad[1:-1, 1:-1, :-2])])
    summed = jnp.sum(corners(nodes).reshape((3, 8, count_z, count_y, count_x)), axis=1)
    whole = jnp.floor_divide(summed, 8 * quantum)
    fraction = (summed - whole * (8 * quantum)).astype(jnp.float32) / (8.0 * quantum)
    anchor_z = jnp.arange(count_z, dtype=jnp.int32) * ELEM
    anchor_y = jnp.arange(count_y, dtype=jnp.int32) * ELEM
    anchor_x = jnp.arange(count_x, dtype=jnp.int32) * ELEM
    start_z = (anchor_z[:, None, None] + whole[0] + ELEM).reshape(-1).astype(jnp.int32)
    start_y = (anchor_y[None, :, None] + whole[1] + ELEM).reshape(-1).astype(jnp.int32)
    start_x = (anchor_x[None, None, :] + whole[2] + ELEM).reshape(-1).astype(jnp.int32)

    def cutout(first, second, third):
        return lax.dynamic_slice(deformed_pad, (first, second, third), (ELEM + 1, ELEM + 1, ELEM + 1))

    boxes = jax.vmap(cutout, out_axes=3)(start_z, start_y, start_x)
    shares = fraction.reshape((3, -1))
    warped = (1.0 - shares[0]) * boxes[:-1] + shares[0] * boxes[1:]
    warped = (1.0 - shares[1]) * warped[:, :-1] + shares[1] * warped[:, 1:]
    warped = (1.0 - shares[2]) * warped[:, :, :-1] + shares[2] * warped[:, :, 1:]
    mismatch = blocks(image) - warped
    slopes = blocks(gradient)
    shape_fn = weights()
    scale = 1.0 / ELEM ** 2
    rhs = jnp.einsum('cijkn,ai,bj,dk->cabdn', slopes * mismatch, shape_fn, shape_fn, shape_fn, precision=lax.Precision.HIGHEST) * scale
    double = shape_fn[:, None, :] * shape_fn[None, :, :]
    rows_list = []
    for component in range(3):
        rows_list.append(jnp.einsum('dijkn,api,bqj,grk->dabgpqrn', slopes[component] * slopes, double, double, double, precision=lax.Precision.HIGHEST) * scale)
    hessian = jnp.stack(rows_list).reshape((3, 3, 2, 2, 2, 2, 2, 2, count_z, count_y, count_x))
    return assemble(rhs.reshape((3, 2, 2, 2, count_z, count_y, count_x))), hessian


def apply_local(hessian, field):
    values = corners(field)
    result = jnp.einsum('cdabgpqrxyz,dpqrxyz->cabgxyz', hessian, values, precision=lax.Precision.HIGHEST)
    return assemble(result)


def unique_nodes(copies):
    for axis, (groups, elems) in enumerate(((N_GZ, EZ), (N_GY, EY), (N_GX, EX))):
        index = np.concatenate([(np.arange(groups)[:, None] * (elems + 1) + np.arange(elems)[None, :]).ravel(), np.array([groups * (elems + 1) - 1])])
        copies = jnp.take(copies, jnp.asarray(index, dtype=jnp.int32), axis=axis + 1)
    return copies


def expand_nodes(field):
    for axis, (groups, elems) in enumerate(((N_GZ, EZ), (N_GY, EY), (N_GX, EX))):
        index = (np.arange(groups)[:, None] * elems + np.arange(elems + 1)[None, :]).ravel()
        field = jnp.take(field, jnp.asarray(index, dtype=jnp.int32), axis=axis + 1)
    return field


def reference(ref_image, deformed_image, nodal_disp):
    nodes = unique_nodes(nodal_disp)
    ref_pad = jnp.pad(ref_image, 1)
    deformed_pad = jnp.pad(deformed_image, ELEM)
    layers = NZ // ELEM
    zero = jnp.zeros((), jnp.int32)

    def layer(index):
        ref_slab = lax.dynamic_slice(ref_pad, (index * ELEM, zero, zero), (ELEM + 2, NY + 2, NX + 2))
        deformed_slab = lax.dynamic_slice(deformed_pad, (index * ELEM, zero, zero), (3 * ELEM, NY + 2 * ELEM, NX + 2 * ELEM))
        node_slab = lax.dynamic_slice(nodes, (zero, index, zero, zero), (3, 2, NY // ELEM + 1, NX // ELEM + 1))
        return element_terms(ref_slab, deformed_slab, node_slab)

    rhs_layers, hess_layers = lax.map(layer, jnp.arange(layers, dtype=jnp.int32))
    rhs = jnp.pad(jnp.moveaxis(rhs_layers[:, :, 0], 0, 1), ((0, 0), (0, 1), (0, 0), (0, 0)))
    rhs = rhs + jnp.pad(jnp.moveaxis(rhs_layers[:, :, 1], 0, 1), ((0, 0), (1, 0), (0, 0), (0, 0)))
    hessian = jnp.moveaxis(hess_layers[..., 0, :, :], 0, 8)

    def operator(field):
        return apply_local(hessian, field) + damping * field

    solution = jnp.zeros_like(rhs)
    residual, direction = rhs, rhs
    norm_now = jnp.sum(residual * residual)
    for step in range(CGSTEPS):
        image = operator(direction)
        alpha = norm_now / jnp.sum(direction * image)
        solution = solution + alpha * direction
        residual = residual - alpha * image
        norm_next = jnp.sum(residual * residual)
        direction = residual + (norm_next / norm_now) * direction
        norm_now = norm_next
    return expand_nodes(float(quantum) * solution), expand_nodes(residual)
```

```python
import functools

import jax
import jax.numpy as jnp
import numpy as np
from jax import lax
from jax.experimental import pallas as pl
from jax.experimental.pallas import tpu as pltpu
from jax.sharding import PartitionSpec as P

ELEM = 16
CGSTEPS = 8
QUANTUM = 64
DAMPING = 0.5
LANES = 128
SLOTS = LANES // ELEM
PAIRS = ((0, 0), (0, 1), (0, 2), (1, 1), (1, 2), (2, 2))
PAIR_OF = ((0, 1, 2), (1, 3, 4), (2, 4, 5))
GROUP = 14
GROUPS = 4

POSITION = (np.arange(ELEM) + 0.5) / ELEM
LINEAR = np.stack([1.0 - POSITION, POSITION])
SQUARED = np.stack([LINEAR[0] * LINEAR[0], LINEAR[0] * LINEAR[1], LINEAR[1] * LINEAR[1]])


def lane_of(shape):
    return lax.broadcasted_iota(jnp.int32, shape, len(shape) - 1)


def pack_face(load, first):
    rows = load(0).shape[0]
    slot = lane_of((rows, LANES)) // ELEM
    per = ELEM // SLOTS
    packed = []
    for part in range(per):
        total = load(part)
        total = pltpu.roll(total, (-first) % LANES, 1) if first else total
        for group in range(1, SLOTS):
            piece = pltpu.roll(load(group * per + part), (ELEM * group - first) % LANES, 1)
            total = jnp.where(slot == group, piece, total)
        packed.append(total)
    return packed


def pack_kernel(deformed_ref, ref_ref, to_low_ref, to_high_ref, ref_low_ref, ref_high_ref):
    for first, out, ref_out in ((0, to_low_ref, ref_low_ref), (LANES - ELEM, to_high_ref, ref_high_ref)):
        for brick in range(deformed_ref.shape[0] // ELEM):
            for part, value in enumerate(
                pack_face(lambda z, brick=brick: deformed_ref[brick * ELEM + z], first)
            ):
                out[brick, part] = value
        for part, value in enumerate(pack_face(lambda z: ref_ref[z], first)):
            ref_out[part] = value


def element_kernel(
    nodes_ref, wide_ref, from_low_ref, from_high_ref, image_ref, z_low_ref, z_high_ref,
    y_low_ref, y_high_ref, x_low_ref, x_high_ref, wy_ref, wx_ref, out_ref,
    low_ref, high_ref, ref_ref, warp_ref, u_ref,
):
    size_z, size_y, size_x = image_ref.shape
    count_y, count_x = size_y // ELEM, size_x // ELEM
    per = ELEM // SLOTS
    rows_wide = wide_ref.shape[1]
    lane_wide = lane_of((rows_wide, LANES))
    lane_y = lane_of((size_y, LANES))

    def spread(z, carry):
        brick, inner = z // ELEM, z % ELEM
        group, part = inner // per, inner % per
        centre = wide_ref[z]
        low = pltpu.roll(from_low_ref[brick, part], LANES - ELEM - ELEM * group, 1)
        low_ref[z] = jnp.where(lane_wide >= LANES - ELEM, low, centre)
        high = pltpu.roll(from_high_ref[brick, part], (LANES - ELEM * group) % LANES, 1)
        high_ref[z] = jnp.where(lane_wide < ELEM, high, centre)
        return carry

    lax.fori_loop(0, wide_ref.shape[0], spread, 0)

    ref_ref[0, 8 : 8 + size_y] = z_low_ref[...]
    ref_ref[size_z + 1, 8 : 8 + size_y] = z_high_ref[...]
    for z in range(size_z):
        ref_ref[z + 1, 0:8] = y_low_ref[z]
        ref_ref[z + 1, 8 : 8 + size_y] = image_ref[z]
        ref_ref[z + 1, 8 + size_y : 16 + size_y] = y_high_ref[z]

    u_ref[...] = jnp.zeros_like(u_ref)
    lane_16 = lane_of((ELEM, LANES))
    lane_8 = lane_of((8, LANES))

    def row(ey, carry):
        base = pl.multiple_of(ey * ELEM, ELEM)

        def element(source, ex):
            starts, shares = [], []
            for c in range(3):
                total = 0
                for offset in range(8):
                    total = total + nodes_ref[
                        c, offset >> 2, ey + (offset >> 1 & 1), ex + (offset & 1)
                    ]
                starts.append((total >> 9) + ELEM)
                shares.append((total & 511).astype(jnp.float32) * (1.0 / (8 * QUANTUM)))
            sz, sy, sx = starts
            fz, fy, fx = shares
            ys = base + sy
            back = (2 * LANES + ELEM - sx) % LANES
            back_next = (2 * LANES + ELEM - 1 - sx) % LANES
            mine = lane_16 // ELEM == ex

            def plane(z):
                return (1.0 - fy) * source[sz + z, pl.ds(ys, ELEM), :] + fy * source[
                    sz + z, pl.ds(ys + 1, ELEM), :
                ]

            before = plane(0)
            for z in range(ELEM):
                after = plane(z + 1)
                mixed = (1.0 - fz) * before + fz * after
                before = after
                value = (1.0 - fx) * pltpu.roll(mixed, back, 1) + fx * pltpu.roll(
                    mixed, back_next, 1
                )
                warp_ref[z] = jnp.where(mine, value, warp_ref[z])

        element(low_ref, 0)

        def middle(ex, carry):
            element(wide_ref, ex)
            return carry

        lax.fori_loop(1, count_x - 1, middle, 0)
        element(high_ref, count_x - 1)

        sums = []
        for half in range(ELEM // 8):
            squares = [[None] * 3 for _ in PAIRS]
            loads = [[None] * 2 for _ in range(3)]
            top = base + 8 * half
            for z in range(ELEM):
                here = ref_ref[z + 1, pl.ds(pl.multiple_of(top + 8, 8), 8), :]
                group, part = z // per, z % per
                slopes = [
                    0.5
                    * (
                        ref_ref[z + 2, pl.ds(pl.multiple_of(top + 8, 8), 8), :]
                        - ref_ref[z, pl.ds(pl.multiple_of(top + 8, 8), 8), :]
                    ),
                    0.5
                    * (
                        ref_ref[z + 1, pl.ds(top + 9, 8), :] - ref_ref[z + 1, pl.ds(top + 7, 8), :]
                    ),
                ]
                at = pl.multiple_of(top, 8)
                left = jnp.where(
                    lane_8 == 0,
                    pltpu.roll(x_low_ref[part, pl.ds(at, 8), :], (LANES - ELEM * group - ELEM + 1) % LANES, 1),
                    pltpu.roll(here, 1, 1),
                )
                right = jnp.where(
                    lane_8 == LANES - 1,
                    pltpu.roll(x_high_ref[part, pl.ds(at, 8), :], (LANES - 1 - ELEM * group) % LANES, 1),
                    pltpu.roll(here, LANES - 1, 1),
                )
                slopes.append(0.5 * (right - left))
                mismatch = here - warp_ref[z, 8 * half : 8 * half + 8, :]
                for index, (c, d) in enumerate(PAIRS):
                    product = slopes[c] * slopes[d]
                    for s in range(3):
                        term = float(SQUARED[s, z]) * product
                        squares[index][s] = term if z == 0 else squares[index][s] + term
                for c in range(3):
                    product = slopes[c] * mismatch
                    for a in range(2):
                        term = float(LINEAR[a, z]) * product
                        loads[c][a] = term if z == 0 else loads[c][a] + term
            sums.append((squares, loads))
        for half in range(2):
            squares, loads = sums[half]
        for index in range(len(PAIRS)):
            for s in range(3):
                for t in range(3):
                    total = sum(
                        sums[half][0][index][s] * wy_ref[t, 8 * half : 8 * half + 8, :]
                        for half in range(2)
                    )
                    kind = index * 9 + s * 3 + t
                    u_ref[pl.ds(kind * count_y + ey, 1), :] = jnp.sum(total, axis=0, keepdims=True)
        for c in range(3):
            for a in range(2):
                for b in range(2):
                    total = sum(
                        sums[half][1][c][a] * wy_ref[3 + b, 8 * half : 8 * half + 8, :]
                        for half in range(2)
                    )
                    kind = GROUP * GROUPS + c * 4 + a * 2 + b
                    u_ref[pl.ds(kind * count_y + ey, 1), :] = jnp.sum(total, axis=0, keepdims=True)
        return carry

    lax.fori_loop(0, count_y, row, 0)

    rows = GROUP * count_y
    total = 0.0
    for group in range(GROUPS + 1):
        total = total + jnp.dot(
            u_ref[group * rows : (group + 1) * rows, :],
            wx_ref[group],
            precision=lax.Precision.HIGHEST,
            preferred_element_type=jnp.float32,
        )
    out_ref[...] = total


def cg_kernel(axes, gathered_ref, update_ref, residual_ref, m_ref, s_ref, r_ref, d_ref):
    count_x, count_y, rows = axes
    places, groups_y = gathered_ref.shape[0], gathered_ref.shape[1]
    total_y = groups_y * count_y
    elems_x = lax.axis_size("gx") * count_x
    shape = (total_y, LANES)
    lane = lane_of(shape)
    line = lax.broadcasted_iota(jnp.int32, shape, 0)
    slot = lane // count_x
    per = 8 // count_y

    def unpack(pair, carry):
        at = pl.multiple_of(pair * 8, 8)
        tiles = [
            [gathered_ref[j, iy, pl.ds(at, 8), :] for iy in range(groups_y)] for j in range(places)
        ]
        for half in range(per):
            values = [
                jnp.concatenate(
                    [tile[half * count_y : (half + 1) * count_y] for tile in tiles[j]], axis=0
                )
                for j in range(places)
            ]
            step = 1
            while step < places:
                bit = (slot // step) % 2 == 0
                fresh = list(values)
                for j in range(places):
                    if (j // step) % 2 == 0:
                        first, second = values[j], values[j + step]
                        fresh[j] = jnp.where(bit, first, pltpu.roll(second, step * count_x, 1))
                        fresh[j + step] = jnp.where(
                            bit, pltpu.roll(first, LANES - step * count_x, 1), second
                        )
                values = fresh
                step *= 2
            for high in range(places):
                m_ref[high * GROUP + pair * per + half] = values[high]
        return carry

    lax.fori_loop(0, GROUP // per, unpack, 0)

    edge = {
        2: (lane % elems_x == 0, lane % elems_x == elems_x - 1, 1, 1),
        1: (line == 0, line == total_y - 1, 1, 0),
        0: (lane < elems_x, lane >= LANES - elems_x, elems_x, 1),
    }
    corner_list = [(a, b, g) for a in range(2) for b in range(2) for g in range(2)]
    keys = [(c,) + k for c in range(3) for k in corner_list]
    position = {key: index for index, key in enumerate(keys)}
    one = jnp.ones(shape, jnp.float32)
    own = {}
    for corner in corner_list:
        mask = one
        for dim in range(3):
            if corner[dim]:
                mask = jnp.where(edge[dim][1], mask, 0.0)
        own[corner] = mask

    def assemble(parts):
        for dim in range(3):
            first, last, shift, axis = edge[dim]
            extent = shape[axis]
            fresh = {}
            for key in keys:
                if key[1 + dim] == 0:
                    other = key[: 1 + dim] + (1,) + key[2 + dim :]
                    low, high = parts[key], parts[other]
                    fresh[key] = low + jnp.where(first, 0.0, pltpu.roll(high, shift, axis))
                    fresh[other] = high + jnp.where(last, 0.0, pltpu.roll(low, extent - shift, axis))
            parts = fresh
        return parts

    def squares(parts):
        total = {}
        for corner in corner_list:
            total[corner] = sum(parts[(c,) + corner] * parts[(c,) + corner] for c in range(3))
        return sum(total[corner] * own[corner] for corner in corner_list)

    parts = {}
    for c, a, b, g in keys:
        parts[c, a, b, g] = m_ref[(3 * GROUPS + g) * GROUP + c * 4 + a * 2 + b]
    parts = assemble(parts)
    for key in keys:
        s_ref[position[key]] = jnp.zeros(shape, jnp.float32)
        r_ref[position[key]] = parts[key]
        d_ref[position[key]] = parts[key]

    def step(index, norm_now):
        d = {key: d_ref[position[key]] for key in keys}
        image = {key: None for key in keys}
        for p, (first, second) in enumerate(PAIRS):
            orders = ((first, second),) if first == second else ((first, second), (second, first))
            for s in range(3):
                for t in range(3):
                    for u in range(3):
                        kind = p * 9 + s * 3 + t
                        value = m_ref[((kind // GROUP) * 3 + u) * GROUP + kind % GROUP]
                        for c, e in orders:
                            for a, b, g in corner_list:
                                q = (s - a, t - b, u - g)
                                if min(q) < 0 or max(q) > 1:
                                    continue
                                term = value * d[(e,) + q]
                                key = (c, a, b, g)
                                image[key] = term if image[key] is None else image[key] + term
        dots = sum(image[key] * d[key] for key in keys) + DAMPING * squares(d)
        alpha = norm_now / jnp.sum(dots)
        image = assemble(image)
        residual = {}
        for key in keys:
            at = position[key]
            s_ref[at] = s_ref[at] + alpha * d[key]
            residual[key] = r_ref[at] - alpha * (image[key] + DAMPING * d[key])
            r_ref[at] = residual[key]
        norm_next = jnp.sum(squares(residual))
        beta = norm_next / norm_now
        for key in keys:
            d_ref[position[key]] = residual[key] + beta * d[key]
        return norm_next

    start = {key: r_ref[position[key]] for key in keys}
    lax.fori_loop(0, CGSTEPS, step, jnp.sum(squares(start)))

    place = lax.axis_index("gz") * lax.axis_size("gx") + lax.axis_index("gx")
    first_lane = place * count_x
    first_line = lax.axis_index("gy") * count_y
    last_lane = (first_lane + count_x) % LANES
    last_line = (first_line + count_y) % total_y
    for source, out, scale in ((s_ref, update_ref, float(QUANTUM)), (r_ref, residual_ref, 1.0)):
        for c in range(3):
            for a in range(2):
                merged = []
                for b in range(2):
                    merged.append(
                        jnp.where(
                            lane == last_lane,
                            pltpu.roll(source[position[c, a, b, 1]], 1, 1),
                            source[position[c, a, b, 0]],
                        )
                    )
                value = jnp.where(line == last_line, pltpu.roll(merged[1], 1, 0), merged[0])
                value = pltpu.roll(value, (LANES - first_lane) % LANES, 1)
                value = pltpu.roll(value, (total_y - first_line) % total_y, 0)
                out[c, a] = scale * value[: count_y + 1, : count_x + 1]


def shifted(block, axis):
    count = lax.axis_size(axis)
    return [(i, i + 1) for i in range(count - 1)], [(i + 1, i) for i in range(count - 1)]


def exchange(to_low, to_high, axis):
    forward, backward = shifted(None, axis)
    return lax.ppermute(to_high, axis, forward), lax.ppermute(to_low, axis, backward)


def x_weights(count_x):
    table = np.zeros((GROUPS + 1, LANES, LANES), np.float32)
    scale = 1.0 / ELEM**2
    for group in range(GROUPS):
        for u in range(3):
            for k in range(count_x):
                column = (group * 3 + u) * count_x + k
                table[group, k * ELEM : (k + 1) * ELEM, column] = SQUARED[u] * scale
    for d in range(2):
        for k in range(count_x):
            column = (3 * GROUPS + d) * count_x + k
            table[GROUPS, k * ELEM : (k + 1) * ELEM, column] = LINEAR[d] * scale
    return jnp.asarray(table)


def y_weights():
    table = np.concatenate([SQUARED, LINEAR]).astype(np.float32)
    return jnp.asarray(np.broadcast_to(table[:, :, None], table.shape + (LANES,)))


VMEM = pl.BlockSpec(memory_space=pltpu.VMEM)
SMEM = pl.BlockSpec(memory_space=pltpu.SMEM)
PARAMS = pltpu.CompilerParams(vmem_limit_bytes=48 * 2**20)


def per_device(ref_image, deformed_image, nodal_disp):
    size_z, size_y, size_x = ref_image.shape
    count_y, count_x = size_y // ELEM, size_x // ELEM
    f32 = jnp.float32
    z_low, z_high = exchange(ref_image[:1], ref_image[-1:], "gz")
    y_low, y_high = exchange(ref_image[:, :8], ref_image[:, -8:], "gy")
    below, above = exchange(deformed_image, deformed_image, "gz")
    tall = jnp.concatenate([below, deformed_image, above], axis=0)
    left, right = exchange(tall[:, :ELEM], tall[:, -ELEM:], "gy")
    wide = jnp.concatenate([left, tall, right], axis=1)
    bricks = wide.shape[0] // ELEM
    per = ELEM // SLOTS
    face = jax.ShapeDtypeStruct((bricks, per, wide.shape[1], LANES), f32)
    ref_face = jax.ShapeDtypeStruct((per, size_y, LANES), f32)
    to_low, to_high, ref_to_low, ref_to_high = pl.pallas_call(
        pack_kernel,
        out_shape=(face, face, ref_face, ref_face),
        in_specs=[VMEM] * 2,
        out_specs=[VMEM] * 4,
        compiler_params=PARAMS,
    )(wide, ref_image)
    from_low, from_high = exchange(to_low, to_high, "gx")
    x_low, x_high = exchange(ref_to_low, ref_to_high, "gx")
    block = pl.pallas_call(
        element_kernel,
        out_shape=jax.ShapeDtypeStruct((GROUP * count_y, LANES), f32),
        in_specs=[SMEM] + [VMEM] * 12,
        out_specs=VMEM,
        scratch_shapes=[
            pltpu.VMEM(wide.shape, f32),
            pltpu.VMEM(wide.shape, f32),
            pltpu.VMEM((size_z + 2, size_y + 16, LANES), f32),
            pltpu.VMEM((ELEM, ELEM, LANES), f32),
            pltpu.VMEM((GROUP * (GROUPS + 1) * count_y, LANES), f32),
        ],
        compiler_params=PARAMS,
    )(
        nodal_disp, wide, from_low, from_high, ref_image, z_low[0], z_high[0],
        y_low, y_high, x_low, x_high, y_weights(), x_weights(count_x),
    )
    gathered = lax.all_gather(block, ("gz", "gx", "gy"), axis=0)
    groups = lax.axis_size("gz") * lax.axis_size("gx")
    gathered = gathered.reshape((groups, lax.axis_size("gy")) + block.shape)
    total_y = lax.axis_size("gy") * count_y
    fields = pltpu.VMEM((24, total_y, LANES), f32)
    nodes_out = jax.ShapeDtypeStruct(nodal_disp.shape, f32)
    return pl.pallas_call(
        functools.partial(cg_kernel, (count_x, count_y, block.shape[0])),
        out_shape=(nodes_out, nodes_out),
        in_specs=[VMEM],
        out_specs=[VMEM] * 2,
        scratch_shapes=[pltpu.VMEM((groups * GROUP, total_y, LANES), f32), fields, fields, fields],
        compiler_params=PARAMS,
    )(gathered)


def solution(mesh):
    in_specs = (P("gz", "gy", "gx"), P("gz", "gy", "gx"), P(None, "gz", "gy", "gx"))
    out_specs = (P(None, "gz", "gy", "gx"), P(None, "gz", "gy", "gx"))
    return jax.shard_map(
        per_device, mesh=mesh, in_specs=in_specs, out_specs=out_specs, check_vma=False
    )
```

```python
import functools

import jax
import jax.numpy as jnp
import numpy as np
from jax import lax
from jax.experimental import pallas as pl
from jax.experimental.pallas import tpu as pltpu
from jax.sharding import PartitionSpec as P

ELEM = 16
CGSTEPS = 8
QUANTUM = 64
DAMPING = 0.5
LANES = 128
SLOTS = LANES // ELEM
PAIRS = ((0, 0), (0, 1), (0, 2), (1, 1), (1, 2), (2, 2))
PAIR_OF = ((0, 1, 2), (1, 3, 4), (2, 4, 5))
GROUP = 14
GROUPS = 4

POSITION = (np.arange(ELEM) + 0.5) / ELEM
LINEAR = np.stack([1.0 - POSITION, POSITION])
SQUARED = np.stack([LINEAR[0] * LINEAR[0], LINEAR[0] * LINEAR[1], LINEAR[1] * LINEAR[1]])


def lane_of(shape):
    return lax.broadcasted_iota(jnp.int32, shape, len(shape) - 1)


def pack_face(load, first):
    rows = load(0).shape[0]
    slot = lane_of((rows, LANES)) // ELEM
    per = ELEM // SLOTS
    packed = []
    for part in range(per):
        total = load(part)
        total = pltpu.roll(total, (-first) % LANES, 1) if first else total
        for group in range(1, SLOTS):
            piece = pltpu.roll(load(group * per + part), (ELEM * group - first) % LANES, 1)
            total = jnp.where(slot == group, piece, total)
        packed.append(total)
    return packed


MESH = pl.DeviceIdType.MESH


def neighbour_barrier(sides):
    barrier = pltpu.get_barrier_semaphore()
    count = 0
    for axis, delta, exists in sides:

        @pl.when(exists)
        def _(axis=axis, delta=delta):
            pl.semaphore_signal(
                barrier, inc=1, device_id={axis: lax.axis_index(axis) + delta}, device_id_type=MESH
            )

        count = count + exists.astype(jnp.int32)
    pl.semaphore_wait(barrier, count)


def halo_kernel(
    image_ref, deformed_ref, wide_ref, from_low_ref, from_high_ref, z_low_ref, z_high_ref,
    y_low_ref, y_high_ref, x_low_ref, x_high_ref,
    to_low_ref, to_high_ref, ref_low_ref, ref_high_ref, send_sem, recv_sem,
):
    size_z, size_y, _ = image_ref.shape
    per = ELEM // SLOTS
    low, high = {}, {}
    for axis in ("gz", "gy", "gx"):
        low[axis] = lax.axis_index(axis) > 0
        high[axis] = lax.axis_index(axis) < lax.axis_size(axis) - 1
    sides = [(axis, -1, low[axis]) for axis in low] + [(axis, 1, high[axis]) for axis in high]
    neighbour_barrier(sides)
    copies = []

    def send(axis, delta, source, target):
        index = len(copies)
        copy = pltpu.make_async_remote_copy(
            src_ref=source,
            dst_ref=target,
            send_sem=send_sem.at[index],
            recv_sem=recv_sem.at[index],
            device_id={axis: lax.axis_index(axis) + delta},
            device_id_type=MESH,
        )
        sends, receives = (high[axis], low[axis]) if delta > 0 else (low[axis], high[axis])
        copies.append((copy, sends))

        @pl.when(sends)
        def _():
            copy.start()

        def arrive():
            @pl.when(receives)
            def _():
                copy.wait_recv()

        def blank(*refs):
            @pl.when(jnp.logical_not(receives))
            def _():
                for ref in refs:
                    ref[...] = jnp.zeros(ref.shape, ref.dtype)

        arrive.blank = blank
        return arrive

    rows = pl.ds(ELEM, size_y)
    below, above = pl.ds(0, ELEM), pl.ds(2 * ELEM, ELEM)
    waits = {}
    waits["z", 0] = send("gz", 1, deformed_ref, wide_ref.at[below, rows])
    waits["z", 2] = send("gz", -1, deformed_ref, wide_ref.at[above, rows])
    middle = pl.ds(ELEM, ELEM)
    first_rows, last_rows = pl.ds(0, ELEM), pl.ds(size_y - ELEM, ELEM)
    into_low, into_high = pl.ds(0, ELEM), pl.ds(ELEM + size_y, ELEM)
    center = [
        send("gy", 1, deformed_ref.at[:, last_rows], wide_ref.at[middle, into_low]),
        send("gy", -1, deformed_ref.at[:, first_rows], wide_ref.at[middle, into_high]),
    ]
    for value, face in ((0, ref_low_ref), (LANES - ELEM, ref_high_ref)):
        for part, packed in enumerate(pack_face(lambda z: image_ref[z], value)):
            face[part] = packed
    others = [
        send("gx", 1, ref_high_ref, x_low_ref),
        send("gx", -1, ref_low_ref, x_high_ref),
        send("gz", 1, image_ref.at[size_z - 1], z_low_ref),
        send("gz", -1, image_ref.at[0], z_high_ref),
        send("gy", 1, image_ref.at[:, pl.ds(size_y - 8, 8)], y_low_ref),
        send("gy", -1, image_ref.at[:, pl.ds(0, 8)], y_high_ref),
    ]
    for arrive, ref in zip(
        others, (x_low_ref, x_high_ref, z_low_ref, z_high_ref, y_low_ref, y_high_ref)
    ):
        arrive.blank(ref)
    waits["z", 0].blank(wide_ref.at[below, rows])
    waits["z", 2].blank(wide_ref.at[above, rows])
    wide_ref[middle, rows] = deformed_ref[...]

    def x_faces(brick, arrivals):
        depth = pl.ds(brick * ELEM, ELEM)
        arrivals[0].blank(wide_ref.at[depth, into_low])
        arrivals[1].blank(wide_ref.at[depth, into_high])
        for arrive in arrivals:
            arrive()
        for first, face in ((0, to_low_ref), (LANES - ELEM, to_high_ref)):
            for part, packed in enumerate(
                pack_face(lambda z: wide_ref[brick * ELEM + z], first)
            ):
                face[brick, part] = packed
        pair = [
            send("gx", 1, to_high_ref.at[brick], from_low_ref.at[brick]),
            send("gx", -1, to_low_ref.at[brick], from_high_ref.at[brick]),
        ]
        pair[0].blank(from_low_ref.at[brick])
        pair[1].blank(from_high_ref.at[brick])
        return pair

    final = x_faces(1, center)
    pending = {}
    for brick in (0, 2):
        waits["z", brick]()
        depth = pl.ds(brick * ELEM, ELEM)
        pending[brick] = [
            send("gy", 1, wide_ref.at[depth, pl.ds(size_y, ELEM)], wide_ref.at[depth, into_low]),
            send("gy", -1, wide_ref.at[depth, pl.ds(ELEM, ELEM)], wide_ref.at[depth, into_high]),
        ]
    for brick in (0, 2):
        final += x_faces(brick, pending[brick])
    for arrive in others + final:
        arrive()
    for copy, sends in copies:

        @pl.when(sends)
        def _(copy=copy):
            copy.wait_send()


HALO_COPIES = 20


def gather_kernel(block_ref, gathered_ref, send_sem, recv_sem):
    size_x, size_y, size_z = gathered_ref.shape[:3]
    ix, iy, iz = lax.axis_index("gx"), lax.axis_index("gy"), lax.axis_index("gz")

    def flip(index, step):
        return index + step - 2 * step * ((index // step) % 2)

    steps = []
    step = size_x // 2
    while step:
        steps.append(step)
        step //= 2
    peers = [{"gz": (iz + hop) % size_z} for hop in range(1, size_z)]
    peers += [{"gy": (iy + hop) % size_y} for hop in range(1, size_y)]
    peers += [{"gx": flip(ix, step)} for step in steps]
    barrier = pltpu.get_barrier_semaphore()
    for peer in peers:
        pl.semaphore_signal(barrier, inc=1, device_id=peer, device_id_type=MESH)
    gathered_ref[ix, iy, iz] = block_ref[...]
    pl.semaphore_wait(barrier, len(peers))
    used = [0]
    sent = []

    def send(source, arriving, peer):
        index = used[0]
        used[0] += 1

        def copy(ref):
            return pltpu.make_async_remote_copy(
                src_ref=ref,
                dst_ref=ref,
                send_sem=send_sem.at[index],
                recv_sem=recv_sem.at[index],
                device_id=peer,
                device_id_type=MESH,
            )

        outgoing = copy(source)
        outgoing.start()
        sent.append(outgoing)
        return copy(arriving)

    phase = []
    for hop in range(1, size_z):
        phase.append(
            send(
                gathered_ref.at[ix, iy, iz],
                gathered_ref.at[ix, iy, (iz + size_z - hop) % size_z],
                peers[hop - 1],
            )
        )
    for copy in phase:
        copy.wait_recv()
    phase = []
    for hop in range(1, size_y):
        phase.append(
            send(
                gathered_ref.at[ix, iy],
                gathered_ref.at[ix, (iy + size_y - hop) % size_y],
                peers[size_z - 2 + hop],
            )
        )
    for copy in phase:
        copy.wait_recv()
    held = [ix]
    for number, step in enumerate(steps):
        phase = [
            send(
                gathered_ref.at[own],
                gathered_ref.at[flip(own, step)],
                peers[size_z + size_y - 2 + number],
            )
            for own in held
        ]
        for copy in phase:
            copy.wait_recv()
        held += [flip(own, step) for own in held]
    for copy in sent:
        copy.wait_send()


def element_kernel(
    nodes_ref, wide_ref, from_low_ref, from_high_ref, image_ref, z_low_ref, z_high_ref,
    y_low_ref, y_high_ref, x_low_ref, x_high_ref, wy_ref, wx_ref, out_ref,
    low_ref, high_ref, ref_ref, warp_ref, u_ref,
):
    size_z, size_y, size_x = image_ref.shape
    count_y, count_x = size_y // ELEM, size_x // ELEM
    per = ELEM // SLOTS
    rows_wide = wide_ref.shape[1]
    lane_wide = lane_of((rows_wide, LANES))
    lane_y = lane_of((size_y, LANES))

    def spread(z, carry):
        brick, inner = z // ELEM, z % ELEM
        group, part = inner // per, inner % per
        centre = wide_ref[z]
        low = pltpu.roll(from_low_ref[brick, part], LANES - ELEM - ELEM * group, 1)
        low_ref[z] = jnp.where(lane_wide >= LANES - ELEM, low, centre)
        high = pltpu.roll(from_high_ref[brick, part], (LANES - ELEM * group) % LANES, 1)
        high_ref[z] = jnp.where(lane_wide < ELEM, high, centre)
        return carry

    lax.fori_loop(0, wide_ref.shape[0], spread, 0)

    ref_ref[0, 8 : 8 + size_y] = z_low_ref[...]
    ref_ref[size_z + 1, 8 : 8 + size_y] = z_high_ref[...]
    for z in range(size_z):
        ref_ref[z + 1, 0:8] = y_low_ref[z]
        ref_ref[z + 1, 8 : 8 + size_y] = image_ref[z]
        ref_ref[z + 1, 8 + size_y : 16 + size_y] = y_high_ref[z]

    u_ref[...] = jnp.zeros_like(u_ref)
    lane_16 = lane_of((ELEM, LANES))
    lane_8 = lane_of((8, LANES))

    def row(ey, carry):
        base = pl.multiple_of(ey * ELEM, ELEM)

        def element(source, ex):
            starts, shares = [], []
            for c in range(3):
                total = 0
                for offset in range(8):
                    total = total + nodes_ref[
                        c, offset >> 2, ey + (offset >> 1 & 1), ex + (offset & 1)
                    ]
                starts.append((total >> 9) + ELEM)
                shares.append((total & 511).astype(jnp.float32) * (1.0 / (8 * QUANTUM)))
            sz, sy, sx = starts
            fz, fy, fx = shares
            ys = base + sy
            back = (2 * LANES + ELEM - sx) % LANES
            back_next = (2 * LANES + ELEM - 1 - sx) % LANES
            mine = lane_16 // ELEM == ex

            def plane(z):
                return (1.0 - fy) * source[sz + z, pl.ds(ys, ELEM), :] + fy * source[
                    sz + z, pl.ds(ys + 1, ELEM), :
                ]

            before = plane(0)
            for z in range(ELEM):
                after = plane(z + 1)
                mixed = (1.0 - fz) * before + fz * after
                before = after
                value = (1.0 - fx) * pltpu.roll(mixed, back, 1) + fx * pltpu.roll(
                    mixed, back_next, 1
                )
                warp_ref[z] = jnp.where(mine, value, warp_ref[z])

        element(low_ref, 0)

        def middle(ex, carry):
            element(wide_ref, ex)
            return carry

        lax.fori_loop(1, count_x - 1, middle, 0)
        element(high_ref, count_x - 1)

        sums = []
        for half in range(ELEM // 8):
            squares = [[None] * 3 for _ in PAIRS]
            loads = [[None] * 2 for _ in range(3)]
            top = base + 8 * half
            for z in range(ELEM):
                here = ref_ref[z + 1, pl.ds(pl.multiple_of(top + 8, 8), 8), :]
                group, part = z // per, z % per
                slopes = [
                    0.5
                    * (
                        ref_ref[z + 2, pl.ds(pl.multiple_of(top + 8, 8), 8), :]
                        - ref_ref[z, pl.ds(pl.multiple_of(top + 8, 8), 8), :]
                    ),
                    0.5
                    * (
                        ref_ref[z + 1, pl.ds(top + 9, 8), :] - ref_ref[z + 1, pl.ds(top + 7, 8), :]
                    ),
                ]
                at = pl.multiple_of(top, 8)
                left = jnp.where(
                    lane_8 == 0,
                    pltpu.roll(x_low_ref[part, pl.ds(at, 8), :], (LANES - ELEM * group - ELEM + 1) % LANES, 1),
                    pltpu.roll(here, 1, 1),
                )
                right = jnp.where(
                    lane_8 == LANES - 1,
                    pltpu.roll(x_high_ref[part, pl.ds(at, 8), :], (LANES - 1 - ELEM * group) % LANES, 1),
                    pltpu.roll(here, LANES - 1, 1),
                )
                slopes.append(0.5 * (right - left))
                mismatch = here - warp_ref[z, 8 * half : 8 * half + 8, :]
                for index, (c, d) in enumerate(PAIRS):
                    product = slopes[c] * slopes[d]
                    for s in range(3):
                        term = float(SQUARED[s, z]) * product
                        squares[index][s] = term if z == 0 else squares[index][s] + term
                for c in range(3):
                    product = slopes[c] * mismatch
                    for a in range(2):
                        term = float(LINEAR[a, z]) * product
                        loads[c][a] = term if z == 0 else loads[c][a] + term
            sums.append((squares, loads))
        for half in range(2):
            squares, loads = sums[half]
        for index in range(len(PAIRS)):
            for s in range(3):
                for t in range(3):
                    total = sum(
                        sums[half][0][index][s] * wy_ref[t, 8 * half : 8 * half + 8, :]
                        for half in range(2)
                    )
                    kind = index * 9 + s * 3 + t
                    u_ref[pl.ds(kind * count_y + ey, 1), :] = jnp.sum(total, axis=0, keepdims=True)
        for c in range(3):
            for a in range(2):
                for b in range(2):
                    total = sum(
                        sums[half][1][c][a] * wy_ref[3 + b, 8 * half : 8 * half + 8, :]
                        for half in range(2)
                    )
                    kind = GROUP * GROUPS + c * 4 + a * 2 + b
                    u_ref[pl.ds(kind * count_y + ey, 1), :] = jnp.sum(total, axis=0, keepdims=True)
        return carry

    lax.fori_loop(0, count_y, row, 0)

    rows = GROUP * count_y
    total = 0.0
    for group in range(GROUPS + 1):
        total = total + jnp.dot(
            u_ref[group * rows : (group + 1) * rows, :],
            wx_ref[group],
            precision=lax.Precision.HIGHEST,
            preferred_element_type=jnp.float32,
        )
    out_ref[...] = total


def cg_kernel(axes, gathered_ref, update_ref, residual_ref, m_ref, s_ref, r_ref, d_ref):
    count_x, count_y, rows = axes
    groups_x, groups_y, groups_z = gathered_ref.shape[:3]
    places = groups_z * groups_x
    total_y = groups_y * count_y
    elems_x = lax.axis_size("gx") * count_x
    shape = (total_y, LANES)
    lane = lane_of(shape)
    line = lax.broadcasted_iota(jnp.int32, shape, 0)
    slot = lane // count_x
    per = 8 // count_y

    def unpack(pair, carry):
        at = pl.multiple_of(pair * 8, 8)
        tiles = [
            [
                gathered_ref[j % groups_x, iy, j // groups_x, pl.ds(at, 8), :]
                for iy in range(groups_y)
            ]
            for j in range(places)
        ]
        for half in range(per):
            values = [
                jnp.concatenate(
                    [tile[half * count_y : (half + 1) * count_y] for tile in tiles[j]], axis=0
                )
                for j in range(places)
            ]
            step = 1
            while step < places:
                bit = (slot // step) % 2 == 0
                fresh = list(values)
                for j in range(places):
                    if (j // step) % 2 == 0:
                        first, second = values[j], values[j + step]
                        fresh[j] = jnp.where(bit, first, pltpu.roll(second, step * count_x, 1))
                        fresh[j + step] = jnp.where(
                            bit, pltpu.roll(first, LANES - step * count_x, 1), second
                        )
                values = fresh
                step *= 2
            for high in range(places):
                m_ref[high * GROUP + pair * per + half] = values[high]
        return carry

    lax.fori_loop(0, GROUP // per, unpack, 0)

    edge = {
        2: (lane % elems_x == 0, lane % elems_x == elems_x - 1, 1, 1),
        1: (line == 0, line == total_y - 1, 1, 0),
        0: (lane < elems_x, lane >= LANES - elems_x, elems_x, 1),
    }
    corner_list = [(a, b, g) for a in range(2) for b in range(2) for g in range(2)]
    keys = [(c,) + k for c in range(3) for k in corner_list]
    position = {key: index for index, key in enumerate(keys)}
    one = jnp.ones(shape, jnp.float32)
    own = {}
    for corner in corner_list:
        mask = one
        for dim in range(3):
            if corner[dim]:
                mask = jnp.where(edge[dim][1], mask, 0.0)
        own[corner] = mask

    def assemble(parts):
        for dim in range(3):
            first, last, shift, axis = edge[dim]
            extent = shape[axis]
            fresh = {}
            for key in keys:
                if key[1 + dim] == 0:
                    other = key[: 1 + dim] + (1,) + key[2 + dim :]
                    low, high = parts[key], parts[other]
                    fresh[key] = low + jnp.where(first, 0.0, pltpu.roll(high, shift, axis))
                    fresh[other] = high + jnp.where(last, 0.0, pltpu.roll(low, extent - shift, axis))
            parts = fresh
        return parts

    def squares(parts):
        total = {}
        for corner in corner_list:
            total[corner] = sum(parts[(c,) + corner] * parts[(c,) + corner] for c in range(3))
        return sum(total[corner] * own[corner] for corner in corner_list)

    parts = {}
    for c, a, b, g in keys:
        parts[c, a, b, g] = m_ref[(3 * GROUPS + g) * GROUP + c * 4 + a * 2 + b]
    parts = assemble(parts)
    for key in keys:
        s_ref[position[key]] = jnp.zeros(shape, jnp.float32)
        r_ref[position[key]] = parts[key]
        d_ref[position[key]] = parts[key]

    def step(index, norm_now):
        d = {key: d_ref[position[key]] for key in keys}
        image = {key: None for key in keys}
        for p, (first, second) in enumerate(PAIRS):
            orders = ((first, second),) if first == second else ((first, second), (second, first))
            for s in range(3):
                for t in range(3):
                    for u in range(3):
                        kind = p * 9 + s * 3 + t
                        value = m_ref[((kind // GROUP) * 3 + u) * GROUP + kind % GROUP]
                        for c, e in orders:
                            for a, b, g in corner_list:
                                q = (s - a, t - b, u - g)
                                if min(q) < 0 or max(q) > 1:
                                    continue
                                term = value * d[(e,) + q]
                                key = (c, a, b, g)
                                image[key] = term if image[key] is None else image[key] + term
        dots = sum(image[key] * d[key] for key in keys) + DAMPING * squares(d)
        alpha = norm_now / jnp.sum(dots)
        image = assemble(image)
        residual = {}
        for key in keys:
            at = position[key]
            s_ref[at] = s_ref[at] + alpha * d[key]
            residual[key] = r_ref[at] - alpha * (image[key] + DAMPING * d[key])
            r_ref[at] = residual[key]
        norm_next = jnp.sum(squares(residual))
        beta = norm_next / norm_now
        for key in keys:
            d_ref[position[key]] = residual[key] + beta * d[key]
        return norm_next

    start = {key: r_ref[position[key]] for key in keys}
    lax.fori_loop(0, CGSTEPS, step, jnp.sum(squares(start)))

    place = lax.axis_index("gz") * lax.axis_size("gx") + lax.axis_index("gx")
    first_lane = place * count_x
    first_line = lax.axis_index("gy") * count_y
    last_lane = (first_lane + count_x) % LANES
    last_line = (first_line + count_y) % total_y
    for source, out, scale in ((s_ref, update_ref, float(QUANTUM)), (r_ref, residual_ref, 1.0)):
        for c in range(3):
            for a in range(2):
                merged = []
                for b in range(2):
                    merged.append(
                        jnp.where(
                            lane == last_lane,
                            pltpu.roll(source[position[c, a, b, 1]], 1, 1),
                            source[position[c, a, b, 0]],
                        )
                    )
                value = jnp.where(line == last_line, pltpu.roll(merged[1], 1, 0), merged[0])
                value = pltpu.roll(value, (LANES - first_lane) % LANES, 1)
                value = pltpu.roll(value, (total_y - first_line) % total_y, 0)
                out[c, a] = scale * value[: count_y + 1, : count_x + 1]


def x_weights(count_x):
    table = np.zeros((GROUPS + 1, LANES, LANES), np.float32)
    scale = 1.0 / ELEM**2
    for group in range(GROUPS):
        for u in range(3):
            for k in range(count_x):
                column = (group * 3 + u) * count_x + k
                table[group, k * ELEM : (k + 1) * ELEM, column] = SQUARED[u] * scale
    for d in range(2):
        for k in range(count_x):
            column = (3 * GROUPS + d) * count_x + k
            table[GROUPS, k * ELEM : (k + 1) * ELEM, column] = LINEAR[d] * scale
    return jnp.asarray(table)


def y_weights():
    table = np.concatenate([SQUARED, LINEAR]).astype(np.float32)
    return jnp.asarray(np.broadcast_to(table[:, :, None], table.shape + (LANES,)))


VMEM = pl.BlockSpec(memory_space=pltpu.VMEM)
SMEM = pl.BlockSpec(memory_space=pltpu.SMEM)
PARAMS = pltpu.CompilerParams(vmem_limit_bytes=48 * 2**20)


def per_device(ref_image, deformed_image, nodal_disp):
    size_z, size_y, size_x = ref_image.shape
    count_y, count_x = size_y // ELEM, size_x // ELEM
    f32 = jnp.float32
    per = ELEM // SLOTS
    wide = jax.ShapeDtypeStruct((3 * ELEM, size_y + 2 * ELEM, LANES), f32)
    face = jax.ShapeDtypeStruct((3, per, size_y + 2 * ELEM, LANES), f32)
    ref_face = jax.ShapeDtypeStruct((per, size_y, LANES), f32)
    plane = jax.ShapeDtypeStruct((size_y, LANES), f32)
    edge = jax.ShapeDtypeStruct((size_z, 8, LANES), f32)
    halos = pl.pallas_call(
        halo_kernel,
        out_shape=(wide, face, face, plane, plane, edge, edge, ref_face, ref_face),
        in_specs=[VMEM] * 2,
        out_specs=[VMEM] * 9,
        scratch_shapes=[
            pltpu.VMEM(face.shape, f32),
            pltpu.VMEM(face.shape, f32),
            pltpu.VMEM(ref_face.shape, f32),
            pltpu.VMEM(ref_face.shape, f32),
            pltpu.SemaphoreType.DMA((HALO_COPIES,)),
            pltpu.SemaphoreType.DMA((HALO_COPIES,)),
        ],
        compiler_params=pltpu.CompilerParams(
            vmem_limit_bytes=48 * 2**20, collective_id=0, has_side_effects=True
        ),
    )(ref_image, deformed_image)
    wide, from_low, from_high, z_low, z_high, y_low, y_high, x_low, x_high = halos
    block = pl.pallas_call(
        element_kernel,
        out_shape=jax.ShapeDtypeStruct((GROUP * count_y, LANES), f32),
        in_specs=[SMEM] + [VMEM] * 12,
        out_specs=VMEM,
        scratch_shapes=[
            pltpu.VMEM(wide.shape, f32),
            pltpu.VMEM(wide.shape, f32),
            pltpu.VMEM((size_z + 2, size_y + 16, LANES), f32),
            pltpu.VMEM((ELEM, ELEM, LANES), f32),
            pltpu.VMEM((GROUP * (GROUPS + 1) * count_y, LANES), f32),
        ],
        compiler_params=PARAMS,
    )(
        nodal_disp, wide, from_low, from_high, ref_image, z_low, z_high,
        y_low, y_high, x_low, x_high, y_weights(), x_weights(count_x),
    )
    sizes = tuple(lax.axis_size(axis) for axis in ("gx", "gy", "gz"))
    groups = sizes[0] * sizes[2]
    copies = sum(sizes) - 3 + sizes[0]
    gathered = pl.pallas_call(
        gather_kernel,
        out_shape=jax.ShapeDtypeStruct(sizes + block.shape, f32),
        in_specs=[VMEM],
        out_specs=VMEM,
        scratch_shapes=[pltpu.SemaphoreType.DMA((copies,)), pltpu.SemaphoreType.DMA((copies,))],
        compiler_params=pltpu.CompilerParams(
            vmem_limit_bytes=48 * 2**20, collective_id=1, has_side_effects=True
        ),
    )(block)
    total_y = lax.axis_size("gy") * count_y
    fields = pltpu.VMEM((24, total_y, LANES), f32)
    nodes_out = jax.ShapeDtypeStruct(nodal_disp.shape, f32)
    return pl.pallas_call(
        functools.partial(cg_kernel, (count_x, count_y, block.shape[0])),
        out_shape=(nodes_out, nodes_out),
        in_specs=[VMEM],
        out_specs=[VMEM] * 2,
        scratch_shapes=[pltpu.VMEM((groups * GROUP, total_y, LANES), f32), fields, fields, fields],
        compiler_params=PARAMS,
    )(gathered)


def solution(mesh):
    in_specs = (P("gz", "gy", "gx"), P("gz", "gy", "gx"), P(None, "gz", "gy", "gx"))
    out_specs = (P(None, "gz", "gy", "gx"), P(None, "gz", "gy", "gx"))
    return jax.shard_map(
        per_device, mesh=mesh, in_specs=in_specs, out_specs=out_specs, check_vma=False
    )
```

```python
import functools

import jax
import jax.numpy as jnp
import numpy as np
from jax import lax
from jax.experimental import pallas as pl
from jax.experimental.pallas import tpu as pltpu
from jax.sharding import PartitionSpec as P

ELEM = 16
CGSTEPS = 8
QUANTUM = 64
DAMPING = 0.5
LANES = 128
SLOTS = LANES // ELEM
PAIRS = ((0, 0), (0, 1), (0, 2), (1, 1), (1, 2), (2, 2))
PAIR_OF = ((0, 1, 2), (1, 3, 4), (2, 4, 5))
GROUP = 12
GROUPS = 5
HALF = 8
CHUNKS = 3 * ELEM // HALF

POSITION = (np.arange(ELEM) + 0.5) / ELEM
LINEAR = np.stack([1.0 - POSITION, POSITION])
SQUARED = np.stack([LINEAR[0] * LINEAR[0], LINEAR[0] * LINEAR[1], LINEAR[1] * LINEAR[1]])


def lane_of(shape):
    return lax.broadcasted_iota(jnp.int32, shape, len(shape) - 1)


def pack_face(load, first):
    total = load(0)
    slot = lane_of(total.shape) // ELEM
    total = pltpu.roll(total, (-first) % LANES, 1) if first else total
    for group in range(1, HALF):
        piece = pltpu.roll(load(group), (ELEM * group - first) % LANES, 1)
        total = jnp.where(slot == group, piece, total)
    return total


def flip(index, step):
    return index + step - 2 * step * ((index // step) % 2)


class Gather:
    def __init__(self, ref, send_sem, recv_sem):
        self.ref, self.sems = ref, (send_sem, recv_sem)
        self.sizes = ref.shape[:3]
        size_x, size_y, size_z = self.sizes
        self.at = ix, iy, iz = tuple(lax.axis_index(axis) for axis in ("gx", "gy", "gz"))
        self.steps = []
        step = size_x // 2
        while step:
            self.steps.append(step)
            step //= 2
        self.z_peers = [{"gz": (iz + hop) % size_z} for hop in range(1, size_z)]
        self.y_peers = [{"gy": (iy + hop) % size_y} for hop in range(1, size_y)]
        self.x_peers = [{"gx": flip(ix, step)} for step in self.steps]
        self.peers = self.z_peers + self.y_peers + self.x_peers
        self.sent, self.phase, self.held = [], [], [ix]

    def send(self, source, arriving, peer):
        index = len(self.sent)

        def copy(ref):
            return pltpu.make_async_remote_copy(
                src_ref=ref,
                dst_ref=ref,
                send_sem=self.sems[0].at[index],
                recv_sem=self.sems[1].at[index],
                device_id=peer,
                device_id_type=MESH,
            )

        outgoing = copy(source)
        outgoing.start()
        self.sent.append(outgoing)
        self.phase.append(copy(arriving))

    def arrive(self):
        for copy in self.phase:
            copy.wait_recv()
        self.phase = []

    def start_z(self):
        (ix, iy, iz), size = self.at, self.sizes[2]
        for hop in range(1, size):
            other = (iz + size - hop) % size
            self.send(self.ref.at[ix, iy, iz], self.ref.at[ix, iy, other], self.z_peers[hop - 1])

    def start_y(self):
        (ix, iy, iz), size = self.at, self.sizes[1]
        for hop in range(1, size):
            other = (iy + size - hop) % size
            self.send(self.ref.at[ix, iy], self.ref.at[ix, other], self.y_peers[hop - 1])

    def start_x(self, number):
        step = self.steps[number]
        for own in self.held:
            self.send(self.ref.at[own], self.ref.at[flip(own, step)], self.x_peers[number])
        self.held = self.held + [flip(own, step) for own in self.held]

    def finish(self):
        for copy in self.sent:
            copy.wait_send()


MESH = pl.DeviceIdType.MESH


def neighbour_barrier(sides, peers):
    barrier = pltpu.get_barrier_semaphore()
    count = len(peers)
    for peer in peers:
        pl.semaphore_signal(barrier, inc=1, device_id=peer, device_id_type=MESH)
    for axis, delta, exists in sides:

        @pl.when(exists)
        def _(axis=axis, delta=delta):
            pl.semaphore_signal(
                barrier, inc=1, device_id={axis: lax.axis_index(axis) + delta}, device_id_type=MESH
            )

        count = count + exists.astype(jnp.int32)
    pl.semaphore_wait(barrier, count)


def moments_row(ey, ref_ref, x_low_ref, x_high_ref, wy_ref, u_ref, count_y):
    lane_8 = lane_of((8, LANES))
    sums = []
    for half in range(ELEM // 8):
        squares = [[None] * 3 for _ in PAIRS]
        at = ey * ELEM + 8 * half
        for z in range(ELEM):
            slopes = slopes_at(z, at, ref_ref, x_low_ref, x_high_ref, lane_8)
            for index, (c, d) in enumerate(PAIRS):
                product = slopes[c] * slopes[d]
                for level in range(3):
                    term = float(SQUARED[level, z]) * product
                    squares[index][level] = term if z == 0 else squares[index][level] + term
        sums.append(squares)
    for index in range(len(PAIRS)):
        for level in range(3):
            for t in range(3):
                total = sum(
                    sums[half][index][level] * wy_ref[t, 8 * half : 8 * half + 8, :]
                    for half in range(2)
                )
                kind = index * 9 + level * 3 + t
                u_ref[pl.ds(kind * count_y + ey, 1), :] = jnp.sum(total, axis=0, keepdims=True)


def slopes_at(z, at, ref_ref, x_low_ref, x_high_ref, lane_8):
    group, part = z % HALF, z // HALF
    at = pl.multiple_of(at, 8)
    row = pl.multiple_of(at + 8, 8)
    here = ref_ref[z + 1, pl.ds(row, 8), :]
    left = jnp.where(
        lane_8 == 0,
        pltpu.roll(x_low_ref[part, pl.ds(at, 8), :], (2 * LANES - ELEM * group - ELEM + 1) % LANES, 1),
        pltpu.roll(here, 1, 1),
    )
    right = jnp.where(
        lane_8 == LANES - 1,
        pltpu.roll(x_high_ref[part, pl.ds(at, 8), :], (LANES - 1 - ELEM * group) % LANES, 1),
        pltpu.roll(here, LANES - 1, 1),
    )
    return (
        0.5 * (ref_ref[z + 2, pl.ds(row, 8), :] - ref_ref[z, pl.ds(row, 8), :]),
        0.5 * (ref_ref[z + 1, pl.ds(at + 9, 8), :] - ref_ref[z + 1, pl.ds(at + 7, 8), :]),
        0.5 * (right - left),
    )


def contract_x(u_ref, wx_ref, rows):
    total = 0.0
    for group in range(wx_ref.shape[0]):
        total = total + jnp.dot(
            u_ref[group * rows : (group + 1) * rows, :],
            wx_ref[group],
            precision=lax.Precision.HIGHEST,
            preferred_element_type=jnp.float32,
        )
    return total


def halo_kernel(
    image_ref, deformed_ref, wy_ref, wx_ref,
    wide_ref, from_low_ref, from_high_ref, ref_ref, x_low_ref, x_high_ref, gathered_ref,
    to_low_ref, to_high_ref, ref_low_ref, ref_high_ref, u_ref,
    z_low_ref, z_high_ref, y_low_ref, y_high_ref, send_sem, recv_sem, gather_send, gather_recv,
):
    size_z, size_y, _ = image_ref.shape
    count_y = size_y // ELEM
    low, high = {}, {}
    for axis in ("gz", "gy", "gx"):
        low[axis] = lax.axis_index(axis) > 0
        high[axis] = lax.axis_index(axis) < lax.axis_size(axis) - 1
    sides = [(axis, -1, low[axis]) for axis in low] + [(axis, 1, high[axis]) for axis in high]
    gather = Gather(gathered_ref, gather_send, gather_recv)
    neighbour_barrier(sides, gather.peers)
    copies = []

    def send(axis, delta, source, target):
        index = len(copies)
        copy = pltpu.make_async_remote_copy(
            src_ref=source,
            dst_ref=target,
            send_sem=send_sem.at[index],
            recv_sem=recv_sem.at[index],
            device_id={axis: lax.axis_index(axis) + delta},
            device_id_type=MESH,
        )
        sends, receives = (high[axis], low[axis]) if delta > 0 else (low[axis], high[axis])
        copies.append((copy, sends))

        @pl.when(sends)
        def _():
            copy.start()

        def arrive():
            @pl.when(receives)
            def _():
                copy.wait_recv()

        def blank(*refs):
            @pl.when(jnp.logical_not(receives))
            def _():
                for ref in refs:
                    ref[...] = jnp.zeros(ref.shape, ref.dtype)

        arrive.blank = blank
        return arrive

    rows = pl.ds(ELEM, size_y)
    middle = pl.ds(ELEM, ELEM)
    first_rows, last_rows = pl.ds(0, ELEM), pl.ds(size_y - ELEM, ELEM)
    into_low, into_high = pl.ds(0, ELEM), pl.ds(ELEM + size_y, ELEM)
    others = [
        send("gz", 1, image_ref.at[size_z - 1], z_low_ref),
        send("gz", -1, image_ref.at[0], z_high_ref),
        send("gy", 1, image_ref.at[:, pl.ds(size_y - 8, 8)], y_low_ref),
        send("gy", -1, image_ref.at[:, pl.ds(0, 8)], y_high_ref),
    ]
    waits = []
    for half in range(ELEM // HALF):
        depth = pl.ds(half * HALF, HALF)
        waits.append(
            [
                send("gz", 1, deformed_ref.at[depth], wide_ref.at[depth, rows]),
                send("gz", -1, deformed_ref.at[depth], wide_ref.at[pl.ds(2 * ELEM + half * HALF, HALF), rows]),
            ]
        )
    center = [
        send("gy", 1, deformed_ref.at[:, last_rows], wide_ref.at[middle, into_low]),
        send("gy", -1, deformed_ref.at[:, first_rows], wide_ref.at[middle, into_high]),
    ]
    for first, face in ((0, ref_low_ref), (LANES - ELEM, ref_high_ref)):
        for half in range(ELEM // HALF):
            face[half] = pack_face(lambda z: image_ref[half * HALF + z], first)
    others += [
        send("gx", 1, ref_high_ref, x_low_ref),
        send("gx", -1, ref_low_ref, x_high_ref),
    ]
    for arrive, ref in zip(
        others, (z_low_ref, z_high_ref, y_low_ref, y_high_ref, x_low_ref, x_high_ref)
    ):
        arrive.blank(ref)
    waits[0][0].blank(wide_ref.at[pl.ds(0, ELEM), rows])
    waits[0][1].blank(wide_ref.at[pl.ds(2 * ELEM, ELEM), rows])
    wide_ref[middle, rows] = deformed_ref[...]
    ref_ref[1 : 1 + size_z, 8 : 8 + size_y] = image_ref[...]
    u_ref[...] = jnp.zeros_like(u_ref)

    final = []

    def x_faces(chunks, arrivals):
        start = pl.ds(chunks[0] * HALF, len(chunks) * HALF)
        arrivals[0].blank(wide_ref.at[start, into_low])
        arrivals[1].blank(wide_ref.at[start, into_high])
        for arrive in arrivals:
            arrive()
        for chunk in chunks:
            for first, face in ((0, to_low_ref), (LANES - ELEM, to_high_ref)):
                face[chunk] = pack_face(lambda z: wide_ref[chunk * HALF + z], first)
            pair = [
                send("gx", 1, to_high_ref.at[chunk], from_low_ref.at[chunk]),
                send("gx", -1, to_low_ref.at[chunk], from_high_ref.at[chunk]),
            ]
            pair[0].blank(from_low_ref.at[chunk])
            pair[1].blank(from_high_ref.at[chunk])
            final.extend(pair)

    def forward_y(half):
        result = []
        for side in range(2):
            waits[half][side]()
            chunk = side * 2 * (ELEM // HALF) + half
            depth = pl.ds(chunk * HALF, HALF)
            result.append(
                (
                    chunk,
                    [
                        send("gy", 1, wide_ref.at[depth, pl.ds(size_y, ELEM)], wide_ref.at[depth, into_low]),
                        send("gy", -1, wide_ref.at[depth, pl.ds(ELEM, ELEM)], wide_ref.at[depth, into_high]),
                    ],
                )
            )
        return result

    for arrive in others:
        arrive()
    ref_ref[0, 8 : 8 + size_y] = z_low_ref[...]
    ref_ref[size_z + 1, 8 : 8 + size_y] = z_high_ref[...]
    ref_ref[1 : 1 + size_z, 0:8] = y_low_ref[...]
    ref_ref[1 : 1 + size_z, 8 + size_y : 16 + size_y] = y_high_ref[...]

    def moments(ey, carry):
        moments_row(ey, ref_ref, x_low_ref, x_high_ref, wy_ref, u_ref, count_y)
        return carry

    lax.fori_loop(0, count_y // 2, moments, 0)
    x_faces((2, 3), center)
    early = forward_y(0)
    lax.fori_loop(count_y // 2, count_y, moments, 0)
    gathered_ref[gather.at[0], gather.at[1], gather.at[2]] = contract_x(
        u_ref, wx_ref, GROUP * count_y
    )
    gather.start_z()
    for chunk, arrivals in early:
        x_faces((chunk,), arrivals)
    late = forward_y(1)
    gather.arrive()
    gather.start_y()
    for chunk, arrivals in late:
        x_faces((chunk,), arrivals)
    gather.arrive()
    for number in range(len(gather.steps)):
        gather.start_x(number)
        gather.arrive()
    for arrive in final:
        arrive()
    gather.finish()
    for copy, sends in copies:

        @pl.when(sends)
        def _(copy=copy):
            copy.wait_send()


HALO_COPIES = 4 + 2 * (ELEM // HALF) + 2 + 2 + 4 * (ELEM // HALF) + 2 * CHUNKS


def gather_kernel(block_ref, gathered_ref, send_sem, recv_sem):
    gather = Gather(gathered_ref, send_sem, recv_sem)
    neighbour_barrier([], gather.peers)
    gathered_ref[gather.at[0], gather.at[1], gather.at[2]] = block_ref[...]
    gather.start_z()
    gather.arrive()
    gather.start_y()
    gather.arrive()
    for number in range(len(gather.steps)):
        gather.start_x(number)
        gather.arrive()
    gather.finish()


def element_kernel(
    nodes_ref, wide_ref, from_low_ref, from_high_ref, ref_ref, x_low_ref, x_high_ref,
    wy_ref, wx_ref, out_ref, low_ref, high_ref, warp_ref, u_ref,
):
    rows_wide = wide_ref.shape[1]
    size_y = rows_wide - 2 * ELEM
    count_y, count_x = size_y // ELEM, LANES // ELEM
    lane_wide = lane_of((rows_wide, LANES))

    def spread(chunk, carry):
        left, right = from_low_ref[chunk], from_high_ref[chunk]
        for group in range(HALF):
            z = chunk * HALF + group
            centre = wide_ref[z]
            low = pltpu.roll(left, (2 * LANES - ELEM - ELEM * group) % LANES, 1)
            low_ref[z] = jnp.where(lane_wide >= LANES - ELEM, low, centre)
            high = pltpu.roll(right, (LANES - ELEM * group) % LANES, 1)
            high_ref[z] = jnp.where(lane_wide < ELEM, high, centre)
        return carry

    lax.fori_loop(0, CHUNKS, spread, 0)

    lane_16 = lane_of((ELEM, LANES))
    lane_8 = lane_of((8, LANES))

    def row(ey, carry):
        base = pl.multiple_of(ey * ELEM, ELEM)

        def element(source, ex):
            starts, shares = [], []
            for c in range(3):
                total = 0
                for offset in range(8):
                    total = total + nodes_ref[
                        c, offset >> 2, ey + (offset >> 1 & 1), ex + (offset & 1)
                    ]
                starts.append((total >> 9) + ELEM)
                shares.append((total & 511).astype(jnp.float32) * (1.0 / (8 * QUANTUM)))
            sz, sy, sx = starts
            fz, fy, fx = shares
            ys = base + sy
            back = (2 * LANES + ELEM - sx) % LANES
            back_next = (2 * LANES + ELEM - 1 - sx) % LANES
            mine = lane_16 // ELEM == ex

            def plane(z):
                return (1.0 - fy) * source[sz + z, pl.ds(ys, ELEM), :] + fy * source[
                    sz + z, pl.ds(ys + 1, ELEM), :
                ]

            before = plane(0)
            for z in range(ELEM):
                after = plane(z + 1)
                mixed = (1.0 - fz) * before + fz * after
                before = after
                value = (1.0 - fx) * pltpu.roll(mixed, back, 1) + fx * pltpu.roll(
                    mixed, back_next, 1
                )
                warp_ref[z] = jnp.where(mine, value, warp_ref[z])

        element(low_ref, 0)

        def middle(ex, carry):
            element(wide_ref, ex)
            return carry

        lax.fori_loop(1, count_x - 1, middle, 0)
        element(high_ref, count_x - 1)

        sums = []
        for half in range(ELEM // 8):
            loads = [[None] * 2 for _ in range(3)]
            at = base + 8 * half
            for z in range(ELEM):
                slopes = slopes_at(z, at, ref_ref, x_low_ref, x_high_ref, lane_8)
                here = ref_ref[z + 1, pl.ds(pl.multiple_of(at + 8, 8), 8), :]
                mismatch = here - warp_ref[z, 8 * half : 8 * half + 8, :]
                for c in range(3):
                    product = slopes[c] * mismatch
                    for a in range(2):
                        term = float(LINEAR[a, z]) * product
                        loads[c][a] = term if z == 0 else loads[c][a] + term
            sums.append(loads)
        for c in range(3):
            for a in range(2):
                for b in range(2):
                    total = sum(
                        sums[half][c][a] * wy_ref[3 + b, 8 * half : 8 * half + 8, :]
                        for half in range(2)
                    )
                    kind = c * 4 + a * 2 + b
                    u_ref[pl.ds(kind * count_y + ey, 1), :] = jnp.sum(total, axis=0, keepdims=True)
        return carry

    lax.fori_loop(0, count_y, row, 0)
    out_ref[...] = contract_x(u_ref, wx_ref, out_ref.shape[0])


def cg_kernel(axes, gathered_ref, loads_ref, update_ref, residual_ref, m_ref, b_ref, s_ref, r_ref, d_ref):
    count_x, count_y = axes
    groups_x, groups_y, groups_z = gathered_ref.shape[:3]
    places = groups_z * groups_x
    total_y = groups_y * count_y
    elems_x = lax.axis_size("gx") * count_x
    shape = (total_y, LANES)
    lane = lane_of(shape)
    line = lax.broadcasted_iota(jnp.int32, shape, 0)
    slot = lane // count_x
    per = 8 // count_y

    def unpack(source, target, lines, pair, carry):
        at = pl.multiple_of(pair * 8, 8)
        tiles = [
            [
                source[j % groups_x, iy, j // groups_x, pl.ds(at, 8), :]
                for iy in range(groups_y)
            ]
            for j in range(places)
        ]
        for half in range(per):
            values = [
                jnp.concatenate(
                    [tile[half * count_y : (half + 1) * count_y] for tile in tiles[j]], axis=0
                )
                for j in range(places)
            ]
            step = 1
            while step < places:
                bit = (slot // step) % 2 == 0
                fresh = list(values)
                for j in range(places):
                    if (j // step) % 2 == 0:
                        first, second = values[j], values[j + step]
                        fresh[j] = jnp.where(bit, first, pltpu.roll(second, step * count_x, 1))
                        fresh[j + step] = jnp.where(
                            bit, pltpu.roll(first, LANES - step * count_x, 1), second
                        )
                values = fresh
                step *= 2
            for high in range(places):
                target[high * lines + pair * per + half] = values[high]
        return carry

    lax.fori_loop(0, GROUP // per, functools.partial(unpack, gathered_ref, m_ref, GROUP), 0)
    unpack(loads_ref, b_ref, per, 0, 0)

    edge = {
        2: (lane % elems_x == 0, lane % elems_x == elems_x - 1, 1, 1),
        1: (line == 0, line == total_y - 1, 1, 0),
        0: (lane < elems_x, lane >= LANES - elems_x, elems_x, 1),
    }
    corner_list = [(a, b, g) for a in range(2) for b in range(2) for g in range(2)]
    keys = [(c,) + k for c in range(3) for k in corner_list]
    position = {key: index for index, key in enumerate(keys)}
    one = jnp.ones(shape, jnp.float32)
    own = {}
    for corner in corner_list:
        mask = one
        for dim in range(3):
            if corner[dim]:
                mask = jnp.where(edge[dim][1], mask, 0.0)
        own[corner] = mask

    def assemble(parts):
        for dim in range(3):
            first, last, shift, axis = edge[dim]
            extent = shape[axis]
            fresh = {}
            for key in keys:
                if key[1 + dim] == 0:
                    other = key[: 1 + dim] + (1,) + key[2 + dim :]
                    low, high = parts[key], parts[other]
                    fresh[key] = low + jnp.where(first, 0.0, pltpu.roll(high, shift, axis))
                    fresh[other] = high + jnp.where(last, 0.0, pltpu.roll(low, extent - shift, axis))
            parts = fresh
        return parts

    def squares(parts):
        total = {}
        for corner in corner_list:
            total[corner] = sum(parts[(c,) + corner] * parts[(c,) + corner] for c in range(3))
        return sum(total[corner] * own[corner] for corner in corner_list)

    parts = {}
    for c, a, b, g in keys:
        kind = c * 4 + a * 2 + b
        parts[c, a, b, g] = b_ref[((kind // per) * 2 + g) * per + kind % per]
    parts = assemble(parts)
    for key in keys:
        s_ref[position[key]] = jnp.zeros(shape, jnp.float32)
        r_ref[position[key]] = parts[key]
        d_ref[position[key]] = parts[key]

    def step(index, norm_now):
        d = {key: d_ref[position[key]] for key in keys}
        image = {key: None for key in keys}
        for p, (first, second) in enumerate(PAIRS):
            orders = ((first, second),) if first == second else ((first, second), (second, first))
            for s in range(3):
                for t in range(3):
                    for u in range(3):
                        kind = p * 9 + s * 3 + t
                        value = m_ref[((kind // GROUP) * 3 + u) * GROUP + kind % GROUP]
                        for c, e in orders:
                            for a, b, g in corner_list:
                                q = (s - a, t - b, u - g)
                                if min(q) < 0 or max(q) > 1:
                                    continue
                                term = value * d[(e,) + q]
                                key = (c, a, b, g)
                                image[key] = term if image[key] is None else image[key] + term
        dots = sum(image[key] * d[key] for key in keys) + DAMPING * squares(d)
        alpha = norm_now / jnp.sum(dots)
        image = assemble(image)
        residual = {}
        for key in keys:
            at = position[key]
            s_ref[at] = s_ref[at] + alpha * d[key]
            residual[key] = r_ref[at] - alpha * (image[key] + DAMPING * d[key])
            r_ref[at] = residual[key]
        norm_next = jnp.sum(squares(residual))
        beta = norm_next / norm_now
        for key in keys:
            d_ref[position[key]] = residual[key] + beta * d[key]
        return norm_next

    start = {key: r_ref[position[key]] for key in keys}
    lax.fori_loop(0, CGSTEPS, step, jnp.sum(squares(start)))

    place = lax.axis_index("gz") * lax.axis_size("gx") + lax.axis_index("gx")
    first_lane = place * count_x
    first_line = lax.axis_index("gy") * count_y
    last_lane = (first_lane + count_x) % LANES
    last_line = (first_line + count_y) % total_y
    for source, out, scale in ((s_ref, update_ref, float(QUANTUM)), (r_ref, residual_ref, 1.0)):
        for c in range(3):
            for a in range(2):
                merged = []
                for b in range(2):
                    merged.append(
                        jnp.where(
                            lane == last_lane,
                            pltpu.roll(source[position[c, a, b, 1]], 1, 1),
                            source[position[c, a, b, 0]],
                        )
                    )
                value = jnp.where(line == last_line, pltpu.roll(merged[1], 1, 0), merged[0])
                value = pltpu.roll(value, (LANES - first_lane) % LANES, 1)
                value = pltpu.roll(value, (total_y - first_line) % total_y, 0)
                out[c, a] = scale * value[: count_y + 1, : count_x + 1]


def x_weights(count_x, weights, groups):
    table = np.zeros((groups, LANES, LANES), np.float32)
    for group in range(groups):
        for u, weight in enumerate(weights):
            for k in range(count_x):
                column = (group * len(weights) + u) * count_x + k
                table[group, k * ELEM : (k + 1) * ELEM, column] = weight / ELEM**2
    return jnp.asarray(table)


def y_weights():
    table = np.concatenate([SQUARED, LINEAR]).astype(np.float32)
    return jnp.asarray(np.broadcast_to(table[:, :, None], table.shape + (LANES,)))


VMEM = pl.BlockSpec(memory_space=pltpu.VMEM)
SMEM = pl.BlockSpec(memory_space=pltpu.SMEM)
PARAMS = pltpu.CompilerParams(vmem_limit_bytes=48 * 2**20)


def per_device(ref_image, deformed_image, nodal_disp):
    size_z, size_y, size_x = ref_image.shape
    count_y, count_x = size_y // ELEM, size_x // ELEM
    f32 = jnp.float32
    per = 8 // count_y
    load_groups = 12 // per
    sizes = tuple(lax.axis_size(axis) for axis in ("gx", "gy", "gz"))
    groups = sizes[0] * sizes[2]
    gather_sems = pltpu.SemaphoreType.DMA((sum(sizes) - 3,))
    moments = jax.ShapeDtypeStruct(sizes + (GROUP * count_y, LANES), f32)
    wide = jax.ShapeDtypeStruct((3 * ELEM, size_y + 2 * ELEM, LANES), f32)
    face = jax.ShapeDtypeStruct((CHUNKS, size_y + 2 * ELEM, LANES), f32)
    ref_face = jax.ShapeDtypeStruct((ELEM // HALF, size_y, LANES), f32)
    padded = jax.ShapeDtypeStruct((size_z + 2, size_y + 16, LANES), f32)
    plane = pltpu.VMEM((size_y, LANES), f32)
    edge = pltpu.VMEM((size_z, 8, LANES), f32)
    by_y = y_weights()
    *halos, gathered = pl.pallas_call(
        halo_kernel,
        out_shape=(wide, face, face, padded, ref_face, ref_face, moments),
        in_specs=[VMEM] * 4,
        out_specs=[VMEM] * 7,
        scratch_shapes=[
            pltpu.VMEM(face.shape, f32),
            pltpu.VMEM(face.shape, f32),
            pltpu.VMEM(ref_face.shape, f32),
            pltpu.VMEM(ref_face.shape, f32),
            pltpu.VMEM((GROUP * GROUPS * count_y, LANES), f32),
            plane,
            plane,
            edge,
            edge,
            pltpu.SemaphoreType.DMA((HALO_COPIES,)),
            pltpu.SemaphoreType.DMA((HALO_COPIES,)),
            gather_sems,
            gather_sems,
        ],
        compiler_params=pltpu.CompilerParams(
            vmem_limit_bytes=48 * 2**20, collective_id=0, has_side_effects=True
        ),
    )(ref_image, deformed_image, by_y, x_weights(count_x, SQUARED, GROUPS))
    block = pl.pallas_call(
        element_kernel,
        out_shape=jax.ShapeDtypeStruct((8, LANES), f32),
        in_specs=[SMEM] + [VMEM] * 8,
        out_specs=VMEM,
        scratch_shapes=[
            pltpu.VMEM(wide.shape, f32),
            pltpu.VMEM(wide.shape, f32),
            pltpu.VMEM((ELEM, ELEM, LANES), f32),
            pltpu.VMEM((12 * count_y, LANES), f32),
        ],
        compiler_params=PARAMS,
    )(nodal_disp, *halos, by_y, x_weights(count_x, LINEAR, load_groups))
    loads = pl.pallas_call(
        gather_kernel,
        out_shape=jax.ShapeDtypeStruct(sizes + block.shape, f32),
        in_specs=[VMEM],
        out_specs=VMEM,
        scratch_shapes=[gather_sems, gather_sems],
        compiler_params=pltpu.CompilerParams(
            vmem_limit_bytes=48 * 2**20, collective_id=1, has_side_effects=True
        ),
    )(block)
    total_y = lax.axis_size("gy") * count_y
    fields = pltpu.VMEM((24, total_y, LANES), f32)
    nodes_out = jax.ShapeDtypeStruct(nodal_disp.shape, f32)
    return pl.pallas_call(
        functools.partial(cg_kernel, (count_x, count_y)),
        out_shape=(nodes_out, nodes_out),
        in_specs=[VMEM] * 2,
        out_specs=[VMEM] * 2,
        scratch_shapes=[
            pltpu.VMEM((groups * GROUP, total_y, LANES), f32),
            pltpu.VMEM((groups * per, total_y, LANES), f32),
            fields,
            fields,
            fields,
        ],
        compiler_params=PARAMS,
    )(gathered, loads)


def solution(mesh):
    in_specs = (P("gz", "gy", "gx"), P("gz", "gy", "gx"), P(None, "gz", "gy", "gx"))
    out_specs = (P(None, "gz", "gy", "gx"), P(None, "gz", "gy", "gx"))
    return jax.shard_map(
        per_device, mesh=mesh, in_specs=in_specs, out_specs=out_specs, check_vma=False
    )
```

```python
import functools

import jax
import jax.numpy as jnp
import numpy as np
from jax import lax
from jax.experimental import pallas as pl
from jax.experimental.pallas import tpu as pltpu
from jax.sharding import PartitionSpec as P

ELEM = 16
CGSTEPS = 8
QUANTUM = 64
DAMPING = 0.5
LANES = 128
SLOTS = LANES // ELEM
PAIRS = ((0, 0), (0, 1), (0, 2), (1, 1), (1, 2), (2, 2))
PAIR_OF = ((0, 1, 2), (1, 3, 4), (2, 4, 5))
GROUP = 12
GROUPS = 5
HALF = 8
CHUNKS = 3 * ELEM // HALF

POSITION = (np.arange(ELEM) + 0.5) / ELEM
LINEAR = np.stack([1.0 - POSITION, POSITION])
SQUARED = np.stack([LINEAR[0] * LINEAR[0], LINEAR[0] * LINEAR[1], LINEAR[1] * LINEAR[1]])


def lane_of(shape):
    return lax.broadcasted_iota(jnp.int32, shape, len(shape) - 1)


def pack_face(load, first):
    total = load(0)
    slot = lane_of(total.shape) // ELEM
    total = pltpu.roll(total, (-first) % LANES, 1) if first else total
    for group in range(1, HALF):
        piece = pltpu.roll(load(group), (ELEM * group - first) % LANES, 1)
        total = jnp.where(slot == group, piece, total)
    return total


def flip(index, step):
    return index + step - 2 * step * ((index // step) % 2)


class Gather:
    def __init__(self, ref, send_sem, recv_sem):
        self.ref, self.sems = ref, (send_sem, recv_sem)
        self.sizes = ref.shape[:3]
        size_x, size_y, size_z = self.sizes
        self.at = ix, iy, iz = tuple(lax.axis_index(axis) for axis in ("gx", "gy", "gz"))
        self.steps = []
        step = size_x // 2
        while step:
            self.steps.append(step)
            step //= 2
        self.z_peers = [{"gz": (iz + hop) % size_z} for hop in range(1, size_z)]
        self.y_peers = [{"gy": (iy + hop) % size_y} for hop in range(1, size_y)]
        self.x_peers = [{"gx": flip(ix, step)} for step in self.steps]
        self.peers = self.z_peers + self.y_peers + self.x_peers
        self.sent, self.phase, self.held = [], [], [ix]

    def send(self, source, arriving, peer):
        index = len(self.sent)

        def copy(ref):
            return pltpu.make_async_remote_copy(
                src_ref=ref,
                dst_ref=ref,
                send_sem=self.sems[0].at[index],
                recv_sem=self.sems[1].at[index],
                device_id=peer,
                device_id_type=MESH,
            )

        outgoing = copy(source)
        outgoing.start()
        self.sent.append(outgoing)
        self.phase.append(copy(arriving))

    def arrive(self):
        for copy in self.phase:
            copy.wait_recv()
        self.phase = []

    def start_z(self):
        (ix, iy, iz), size = self.at, self.sizes[2]
        for hop in range(1, size):
            other = (iz + size - hop) % size
            self.send(self.ref.at[ix, iy, iz], self.ref.at[ix, iy, other], self.z_peers[hop - 1])

    def start_y(self):
        (ix, iy, iz), size = self.at, self.sizes[1]
        for hop in range(1, size):
            other = (iy + size - hop) % size
            self.send(self.ref.at[ix, iy], self.ref.at[ix, other], self.y_peers[hop - 1])

    def start_x(self, number):
        step = self.steps[number]
        for own in self.held:
            self.send(self.ref.at[own], self.ref.at[flip(own, step)], self.x_peers[number])
        self.held = self.held + [flip(own, step) for own in self.held]

    def finish(self):
        for copy in self.sent:
            copy.wait_send()


MESH = pl.DeviceIdType.MESH


def neighbour_barrier(sides, peers):
    barrier = pltpu.get_barrier_semaphore()
    count = len(peers)
    for peer in peers:
        pl.semaphore_signal(barrier, inc=1, device_id=peer, device_id_type=MESH)
    for axis, delta, exists in sides:

        @pl.when(exists)
        def _(axis=axis, delta=delta):
            pl.semaphore_signal(
                barrier, inc=1, device_id={axis: lax.axis_index(axis) + delta}, device_id_type=MESH
            )

        count = count + exists.astype(jnp.int32)
    pl.semaphore_wait(barrier, count)


def ramp(shape, axis):
    index = lax.broadcasted_iota(jnp.int32, shape, axis) % ELEM
    return (index.astype(jnp.float32) + 0.5) * (1.0 / ELEM)


def powers(position, squared):
    rest = 1.0 - position
    if squared:
        return (rest * rest, rest * position, position * position)
    return (rest, position)


def x_weights(group, squared):
    shape = (LANES, LANES)
    count_x = LANES // ELEM
    row, column = (lax.broadcasted_iota(jnp.int32, shape, axis) for axis in (0, 1))
    weights = powers(ramp(shape, 0), squared)
    total = jnp.zeros(shape, jnp.float32)
    for u, weight in enumerate(weights):
        slot = group * len(weights) + u
        mine = jnp.logical_and(column // count_x == slot, row // ELEM == column % count_x)
        total = jnp.where(mine, weight * (1.0 / ELEM**2), total)
    return total


def moments_row(ey, ref_ref, x_low_ref, x_high_ref, u_ref, count_y):
    by_y = powers(ramp((ELEM, LANES), 0), True)
    lane_8 = lane_of((8, LANES))
    sums = []
    for half in range(ELEM // 8):
        squares = [[None] * 3 for _ in PAIRS]
        at = ey * ELEM + 8 * half
        for z in range(ELEM):
            slopes = slopes_at(z, at, ref_ref, x_low_ref, x_high_ref, lane_8)
            for index, (c, d) in enumerate(PAIRS):
                product = slopes[c] * slopes[d]
                for level in range(3):
                    term = float(SQUARED[level, z]) * product
                    squares[index][level] = term if z == 0 else squares[index][level] + term
        sums.append(squares)
    for index in range(len(PAIRS)):
        for level in range(3):
            for t in range(3):
                total = sum(
                    sums[half][index][level] * by_y[t][8 * half : 8 * half + 8, :]
                    for half in range(2)
                )
                kind = index * 9 + level * 3 + t
                u_ref[pl.ds(kind * count_y + ey, 1), :] = jnp.sum(total, axis=0, keepdims=True)


def slopes_at(z, at, ref_ref, x_low_ref, x_high_ref, lane_8):
    group, part = z % HALF, z // HALF
    at = pl.multiple_of(at, 8)
    row = pl.multiple_of(at + 8, 8)
    here = ref_ref[z + 1, pl.ds(row, 8), :]
    left = jnp.where(
        lane_8 == 0,
        pltpu.roll(x_low_ref[part, pl.ds(at, 8), :], (2 * LANES - ELEM * group - ELEM + 1) % LANES, 1),
        pltpu.roll(here, 1, 1),
    )
    right = jnp.where(
        lane_8 == LANES - 1,
        pltpu.roll(x_high_ref[part, pl.ds(at, 8), :], (LANES - 1 - ELEM * group) % LANES, 1),
        pltpu.roll(here, LANES - 1, 1),
    )
    return (
        0.5 * (ref_ref[z + 2, pl.ds(row, 8), :] - ref_ref[z, pl.ds(row, 8), :]),
        0.5 * (ref_ref[z + 1, pl.ds(at + 9, 8), :] - ref_ref[z + 1, pl.ds(at + 7, 8), :]),
        0.5 * (right - left),
    )


def contract_x(u_ref, squared, rows):
    total = 0.0
    for group in range(u_ref.shape[0] // rows):
        total = total + jnp.dot(
            u_ref[group * rows : (group + 1) * rows, :],
            x_weights(group, squared),
            precision=lax.Precision.HIGHEST,
            preferred_element_type=jnp.float32,
        )
    return total


def halo_kernel(
    image_ref, deformed_ref,
    wide_ref, from_low_ref, from_high_ref, ref_ref, x_low_ref, x_high_ref, gathered_ref,
    to_low_ref, to_high_ref, ref_low_ref, ref_high_ref, u_ref,
    z_low_ref, z_high_ref, y_low_ref, y_high_ref, send_sem, recv_sem, gather_send, gather_recv,
):
    size_z, size_y, _ = image_ref.shape
    count_y = size_y // ELEM
    low, high = {}, {}
    for axis in ("gz", "gy", "gx"):
        low[axis] = lax.axis_index(axis) > 0
        high[axis] = lax.axis_index(axis) < lax.axis_size(axis) - 1
    sides = [(axis, -1, low[axis]) for axis in low] + [(axis, 1, high[axis]) for axis in high]
    gather = Gather(gathered_ref, gather_send, gather_recv)
    neighbour_barrier(sides, gather.peers)
    copies = []

    def send(axis, delta, source, target):
        index = len(copies)
        copy = pltpu.make_async_remote_copy(
            src_ref=source,
            dst_ref=target,
            send_sem=send_sem.at[index],
            recv_sem=recv_sem.at[index],
            device_id={axis: lax.axis_index(axis) + delta},
            device_id_type=MESH,
        )
        sends, receives = (high[axis], low[axis]) if delta > 0 else (low[axis], high[axis])
        copies.append((copy, sends))

        @pl.when(sends)
        def _():
            copy.start()

        def arrive():
            @pl.when(receives)
            def _():
                copy.wait_recv()

        def blank(*refs):
            @pl.when(jnp.logical_not(receives))
            def _():
                for ref in refs:
                    ref[...] = jnp.zeros(ref.shape, ref.dtype)

        arrive.blank = blank
        return arrive

    rows = pl.ds(ELEM, size_y)
    middle = pl.ds(ELEM, ELEM)
    first_rows, last_rows = pl.ds(0, ELEM), pl.ds(size_y - ELEM, ELEM)
    into_low, into_high = pl.ds(0, ELEM), pl.ds(ELEM + size_y, ELEM)
    others = [
        send("gz", 1, image_ref.at[size_z - 1], z_low_ref),
        send("gz", -1, image_ref.at[0], z_high_ref),
        send("gy", 1, image_ref.at[:, pl.ds(size_y - 8, 8)], y_low_ref),
        send("gy", -1, image_ref.at[:, pl.ds(0, 8)], y_high_ref),
    ]
    waits = []
    for half in range(ELEM // HALF):
        depth = pl.ds(half * HALF, HALF)
        waits.append(
            [
                send("gz", 1, deformed_ref.at[depth], wide_ref.at[depth, rows]),
                send("gz", -1, deformed_ref.at[depth], wide_ref.at[pl.ds(2 * ELEM + half * HALF, HALF), rows]),
            ]
        )
    center = [
        send("gy", 1, deformed_ref.at[:, last_rows], wide_ref.at[middle, into_low]),
        send("gy", -1, deformed_ref.at[:, first_rows], wide_ref.at[middle, into_high]),
    ]
    for first, face in ((0, ref_low_ref), (LANES - ELEM, ref_high_ref)):
        for half in range(ELEM // HALF):
            face[half] = pack_face(lambda z: image_ref[half * HALF + z], first)
    others += [
        send("gx", 1, ref_high_ref, x_low_ref),
        send("gx", -1, ref_low_ref, x_high_ref),
    ]
    for arrive, ref in zip(
        others, (z_low_ref, z_high_ref, y_low_ref, y_high_ref, x_low_ref, x_high_ref)
    ):
        arrive.blank(ref)
    waits[0][0].blank(wide_ref.at[pl.ds(0, ELEM), rows])
    waits[0][1].blank(wide_ref.at[pl.ds(2 * ELEM, ELEM), rows])
    wide_ref[middle, rows] = deformed_ref[...]
    ref_ref[1 : 1 + size_z, 8 : 8 + size_y] = image_ref[...]
    u_ref[...] = jnp.zeros_like(u_ref)

    final = []

    def x_faces(chunks, arrivals):
        start = pl.ds(chunks[0] * HALF, len(chunks) * HALF)
        arrivals[0].blank(wide_ref.at[start, into_low])
        arrivals[1].blank(wide_ref.at[start, into_high])
        for arrive in arrivals:
            arrive()
        for chunk in chunks:
            for first, face in ((0, to_low_ref), (LANES - ELEM, to_high_ref)):
                face[chunk] = pack_face(lambda z: wide_ref[chunk * HALF + z], first)
            pair = [
                send("gx", 1, to_high_ref.at[chunk], from_low_ref.at[chunk]),
                send("gx", -1, to_low_ref.at[chunk], from_high_ref.at[chunk]),
            ]
            pair[0].blank(from_low_ref.at[chunk])
            pair[1].blank(from_high_ref.at[chunk])
            final.extend(pair)

    def forward_y(half):
        result = []
        for side in range(2):
            waits[half][side]()
            chunk = side * 2 * (ELEM // HALF) + half
            depth = pl.ds(chunk * HALF, HALF)
            result.append(
                (
                    chunk,
                    [
                        send("gy", 1, wide_ref.at[depth, pl.ds(size_y, ELEM)], wide_ref.at[depth, into_low]),
                        send("gy", -1, wide_ref.at[depth, pl.ds(ELEM, ELEM)], wide_ref.at[depth, into_high]),
                    ],
                )
            )
        return result

    for arrive in others:
        arrive()
    ref_ref[0, 8 : 8 + size_y] = z_low_ref[...]
    ref_ref[size_z + 1, 8 : 8 + size_y] = z_high_ref[...]
    ref_ref[1 : 1 + size_z, 0:8] = y_low_ref[...]
    ref_ref[1 : 1 + size_z, 8 + size_y : 16 + size_y] = y_high_ref[...]

    def moments(ey, carry):
        moments_row(ey, ref_ref, x_low_ref, x_high_ref, u_ref, count_y)
        return carry

    lax.fori_loop(0, count_y // 2, moments, 0)
    x_faces((2, 3), center)
    early = forward_y(0)
    lax.fori_loop(count_y // 2, count_y, moments, 0)
    gathered_ref[gather.at[0], gather.at[1], gather.at[2]] = contract_x(
        u_ref, True, GROUP * count_y
    )
    gather.start_z()
    for chunk, arrivals in early:
        x_faces((chunk,), arrivals)
    late = forward_y(1)
    gather.arrive()
    gather.start_y()
    for chunk, arrivals in late:
        x_faces((chunk,), arrivals)
    gather.arrive()
    for number in range(len(gather.steps)):
        gather.start_x(number)
        gather.arrive()
    for arrive in final:
        arrive()
    gather.finish()
    for copy, sends in copies:

        @pl.when(sends)
        def _(copy=copy):
            copy.wait_send()


HALO_COPIES = 4 + 2 * (ELEM // HALF) + 2 + 2 + 4 * (ELEM // HALF) + 2 * CHUNKS


def gather_kernel(block_ref, gathered_ref, send_sem, recv_sem):
    sizes = gathered_ref.shape[:3]
    at = tuple(lax.axis_index(axis) for axis in ("gx", "gy", "gz"))
    hops = [
        (x, y, z)
        for z in range(sizes[2])
        for y in range(sizes[1])
        for x in range(sizes[0])
        if x or y or z
    ]

    def away(hop, sign):
        return tuple((at[i] + sizes[i] + sign * hop[i]) % sizes[i] for i in range(3))

    targets = [away(hop, 1) for hop in hops]
    peers = [dict(zip(("gx", "gy", "gz"), target)) for target in targets]
    neighbour_barrier([], peers)
    outgoing = []
    for index, peer in enumerate(peers):
        copy = pltpu.make_async_remote_copy(
            src_ref=block_ref,
            dst_ref=gathered_ref.at[at],
            send_sem=send_sem.at[index],
            recv_sem=recv_sem.at[index],
            device_id=peer,
            device_id_type=MESH,
        )
        copy.start()
        outgoing.append(copy)
    gathered_ref[at] = block_ref[...]
    for index, hop in enumerate(hops):
        pltpu.make_async_remote_copy(
            src_ref=block_ref,
            dst_ref=gathered_ref.at[away(hop, -1)],
            send_sem=send_sem.at[index],
            recv_sem=recv_sem.at[index],
            device_id=peers[index],
            device_id_type=MESH,
        ).wait_recv()
    for copy in outgoing:
        copy.wait_send()


def element_kernel(
    nodes_ref, wide_ref, from_low_ref, from_high_ref, ref_ref, x_low_ref, x_high_ref,
    out_ref, low_ref, high_ref, warp_ref, u_ref,
):
    rows_wide = wide_ref.shape[1]
    size_y = rows_wide - 2 * ELEM
    count_y, count_x = size_y // ELEM, LANES // ELEM
    lane_wide = lane_of((rows_wide, LANES))

    def spread(chunk, carry):
        left, right = from_low_ref[chunk], from_high_ref[chunk]
        for group in range(HALF):
            z = chunk * HALF + group
            centre = wide_ref[z]
            low = pltpu.roll(left, (2 * LANES - ELEM - ELEM * group) % LANES, 1)
            low_ref[z] = jnp.where(lane_wide >= LANES - ELEM, low, centre)
            high = pltpu.roll(right, (LANES - ELEM * group) % LANES, 1)
            high_ref[z] = jnp.where(lane_wide < ELEM, high, centre)
        return carry

    lax.fori_loop(0, CHUNKS, spread, 0)
    by_y = powers(ramp((ELEM, LANES), 0), False)

    lane_16 = lane_of((ELEM, LANES))
    lane_8 = lane_of((8, LANES))

    def row(ey, carry):
        base = pl.multiple_of(ey * ELEM, ELEM)

        def element(source, ex):
            starts, shares = [], []
            for c in range(3):
                total = 0
                for offset in range(8):
                    total = total + nodes_ref[
                        c, offset >> 2, ey + (offset >> 1 & 1), ex + (offset & 1)
                    ]
                starts.append((total >> 9) + ELEM)
                shares.append((total & 511).astype(jnp.float32) * (1.0 / (8 * QUANTUM)))
            sz, sy, sx = starts
            fz, fy, fx = shares
            ys = base + sy
            back = (2 * LANES + ELEM - sx) % LANES
            back_next = (2 * LANES + ELEM - 1 - sx) % LANES
            mine = lane_16 // ELEM == ex

            def plane(z):
                return (1.0 - fy) * source[sz + z, pl.ds(ys, ELEM), :] + fy * source[
                    sz + z, pl.ds(ys + 1, ELEM), :
                ]

            before = plane(0)
            for z in range(ELEM):
                after = plane(z + 1)
                mixed = (1.0 - fz) * before + fz * after
                before = after
                value = (1.0 - fx) * pltpu.roll(mixed, back, 1) + fx * pltpu.roll(
                    mixed, back_next, 1
                )
                warp_ref[z] = jnp.where(mine, value, warp_ref[z])

        element(low_ref, 0)

        def middle(ex, carry):
            element(wide_ref, ex)
            return carry

        lax.fori_loop(1, count_x - 1, middle, 0)
        element(high_ref, count_x - 1)

        sums = []
        for half in range(ELEM // 8):
            loads = [[None] * 2 for _ in range(3)]
            at = base + 8 * half
            for z in range(ELEM):
                slopes = slopes_at(z, at, ref_ref, x_low_ref, x_high_ref, lane_8)
                here = ref_ref[z + 1, pl.ds(pl.multiple_of(at + 8, 8), 8), :]
                mismatch = here - warp_ref[z, 8 * half : 8 * half + 8, :]
                for c in range(3):
                    product = slopes[c] * mismatch
                    for a in range(2):
                        term = float(LINEAR[a, z]) * product
                        loads[c][a] = term if z == 0 else loads[c][a] + term
            sums.append(loads)
        for c in range(3):
            for a in range(2):
                for b in range(2):
                    total = sum(
                        sums[half][c][a] * by_y[b][8 * half : 8 * half + 8, :]
                        for half in range(2)
                    )
                    kind = c * 4 + a * 2 + b
                    u_ref[pl.ds(kind * count_y + ey, 1), :] = jnp.sum(total, axis=0, keepdims=True)
        return carry

    lax.fori_loop(0, count_y, row, 0)
    out_ref[...] = contract_x(u_ref, False, out_ref.shape[0])


def cg_kernel(axes, gathered_ref, loads_ref, update_ref, residual_ref, m_ref, b_ref, s_ref, r_ref, d_ref):
    count_x, count_y = axes
    groups_x, groups_y, groups_z = gathered_ref.shape[:3]
    places = groups_z * groups_x
    total_y = groups_y * count_y
    elems_x = lax.axis_size("gx") * count_x
    shape = (total_y, LANES)
    lane = lane_of(shape)
    line = lax.broadcasted_iota(jnp.int32, shape, 0)
    slot = lane // count_x
    per = 8 // count_y

    def unpack(source, target, lines, pair, carry):
        at = pl.multiple_of(pair * 8, 8)
        tiles = [
            [
                source[j % groups_x, iy, j // groups_x, pl.ds(at, 8), :]
                for iy in range(groups_y)
            ]
            for j in range(places)
        ]
        for half in range(per):
            values = [
                jnp.concatenate(
                    [tile[half * count_y : (half + 1) * count_y] for tile in tiles[j]], axis=0
                )
                for j in range(places)
            ]
            step = 1
            while step < places:
                bit = (slot // step) % 2 == 0
                fresh = list(values)
                for j in range(places):
                    if (j // step) % 2 == 0:
                        first, second = values[j], values[j + step]
                        fresh[j] = jnp.where(bit, first, pltpu.roll(second, step * count_x, 1))
                        fresh[j + step] = jnp.where(
                            bit, pltpu.roll(first, LANES - step * count_x, 1), second
                        )
                values = fresh
                step *= 2
            for high in range(places):
                target[high * lines + pair * per + half] = values[high]
        return carry

    lax.fori_loop(0, GROUP // per, functools.partial(unpack, gathered_ref, m_ref, GROUP), 0)
    unpack(loads_ref, b_ref, per, 0, 0)

    edge = {
        2: (lane % elems_x == 0, lane % elems_x == elems_x - 1, 1, 1),
        1: (line == 0, line == total_y - 1, 1, 0),
        0: (lane < elems_x, lane >= LANES - elems_x, elems_x, 1),
    }
    corner_list = [(a, b, g) for a in range(2) for b in range(2) for g in range(2)]
    keys = [(c,) + k for c in range(3) for k in corner_list]
    position = {key: index for index, key in enumerate(keys)}
    one = jnp.ones(shape, jnp.float32)
    own = {}
    for corner in corner_list:
        mask = one
        for dim in range(3):
            if corner[dim]:
                mask = jnp.where(edge[dim][1], mask, 0.0)
        own[corner] = mask

    def assemble(parts):
        for dim in range(3):
            first, last, shift, axis = edge[dim]
            extent = shape[axis]
            fresh = {}
            for key in keys:
                if key[1 + dim] == 0:
                    other = key[: 1 + dim] + (1,) + key[2 + dim :]
                    low, high = parts[key], parts[other]
                    fresh[key] = low + jnp.where(first, 0.0, pltpu.roll(high, shift, axis))
                    fresh[other] = high + jnp.where(last, 0.0, pltpu.roll(low, extent - shift, axis))
            parts = fresh
        return parts

    def squares(parts):
        total = {}
        for corner in corner_list:
            total[corner] = sum(parts[(c,) + corner] * parts[(c,) + corner] for c in range(3))
        return sum(total[corner] * own[corner] for corner in corner_list)

    parts = {}
    for c, a, b, g in keys:
        kind = c * 4 + a * 2 + b
        parts[c, a, b, g] = b_ref[((kind // per) * 2 + g) * per + kind % per]
    parts = assemble(parts)
    for key in keys:
        s_ref[position[key]] = jnp.zeros(shape, jnp.float32)
        r_ref[position[key]] = parts[key]
        d_ref[position[key]] = parts[key]

    def step(index, norm_now):
        d = {key: d_ref[position[key]] for key in keys}
        image = {key: None for key in keys}
        for p, (first, second) in enumerate(PAIRS):
            orders = ((first, second),) if first == second else ((first, second), (second, first))
            for s in range(3):
                for t in range(3):
                    for u in range(3):
                        kind = p * 9 + s * 3 + t
                        value = m_ref[((kind // GROUP) * 3 + u) * GROUP + kind % GROUP]
                        for c, e in orders:
                            for a, b, g in corner_list:
                                q = (s - a, t - b, u - g)
                                if min(q) < 0 or max(q) > 1:
                                    continue
                                term = value * d[(e,) + q]
                                key = (c, a, b, g)
                                image[key] = term if image[key] is None else image[key] + term
        dots = sum(image[key] * d[key] for key in keys) + DAMPING * squares(d)
        alpha = norm_now / jnp.sum(dots)
        image = assemble(image)
        residual = {}
        for key in keys:
            at = position[key]
            s_ref[at] = s_ref[at] + alpha * d[key]
            residual[key] = r_ref[at] - alpha * (image[key] + DAMPING * d[key])
            r_ref[at] = residual[key]
        norm_next = jnp.sum(squares(residual))
        beta = norm_next / norm_now
        for key in keys:
            d_ref[position[key]] = residual[key] + beta * d[key]
        return norm_next

    start = {key: r_ref[position[key]] for key in keys}
    lax.fori_loop(0, CGSTEPS, step, jnp.sum(squares(start)))

    place = lax.axis_index("gz") * lax.axis_size("gx") + lax.axis_index("gx")
    first_lane = place * count_x
    first_line = lax.axis_index("gy") * count_y
    last_lane = (first_lane + count_x) % LANES
    last_line = (first_line + count_y) % total_y
    for source, out, scale in ((s_ref, update_ref, float(QUANTUM)), (r_ref, residual_ref, 1.0)):
        for c in range(3):
            for a in range(2):
                merged = []
                for b in range(2):
                    merged.append(
                        jnp.where(
                            lane == last_lane,
                            pltpu.roll(source[position[c, a, b, 1]], 1, 1),
                            source[position[c, a, b, 0]],
                        )
                    )
                value = jnp.where(line == last_line, pltpu.roll(merged[1], 1, 0), merged[0])
                value = pltpu.roll(value, (LANES - first_lane) % LANES, 1)
                value = pltpu.roll(value, (total_y - first_line) % total_y, 0)
                out[c, a] = scale * value[: count_y + 1, : count_x + 1]


VMEM = pl.BlockSpec(memory_space=pltpu.VMEM)
SMEM = pl.BlockSpec(memory_space=pltpu.SMEM)
PARAMS = pltpu.CompilerParams(vmem_limit_bytes=48 * 2**20)


def per_device(ref_image, deformed_image, nodal_disp):
    size_z, size_y, size_x = ref_image.shape
    count_y, count_x = size_y // ELEM, size_x // ELEM
    f32 = jnp.float32
    per = 8 // count_y
    sizes = tuple(lax.axis_size(axis) for axis in ("gx", "gy", "gz"))
    groups = sizes[0] * sizes[2]
    gather_sems = pltpu.SemaphoreType.DMA((sum(sizes) - 3,))
    direct_sems = pltpu.SemaphoreType.DMA((groups * sizes[1] - 1,))
    moments = jax.ShapeDtypeStruct(sizes + (GROUP * count_y, LANES), f32)
    wide = jax.ShapeDtypeStruct((3 * ELEM, size_y + 2 * ELEM, LANES), f32)
    face = jax.ShapeDtypeStruct((CHUNKS, size_y + 2 * ELEM, LANES), f32)
    ref_face = jax.ShapeDtypeStruct((ELEM // HALF, size_y, LANES), f32)
    padded = jax.ShapeDtypeStruct((size_z + 2, size_y + 16, LANES), f32)
    plane = pltpu.VMEM((size_y, LANES), f32)
    edge = pltpu.VMEM((size_z, 8, LANES), f32)
    *halos, gathered = pl.pallas_call(
        halo_kernel,
        out_shape=(wide, face, face, padded, ref_face, ref_face, moments),
        in_specs=[VMEM] * 2,
        out_specs=[VMEM] * 7,
        scratch_shapes=[
            pltpu.VMEM(face.shape, f32),
            pltpu.VMEM(face.shape, f32),
            pltpu.VMEM(ref_face.shape, f32),
            pltpu.VMEM(ref_face.shape, f32),
            pltpu.VMEM((GROUP * GROUPS * count_y, LANES), f32),
            plane,
            plane,
            edge,
            edge,
            pltpu.SemaphoreType.DMA((HALO_COPIES,)),
            pltpu.SemaphoreType.DMA((HALO_COPIES,)),
            gather_sems,
            gather_sems,
        ],
        compiler_params=pltpu.CompilerParams(
            vmem_limit_bytes=48 * 2**20, collective_id=0, has_side_effects=True
        ),
    )(ref_image, deformed_image)
    block = pl.pallas_call(
        element_kernel,
        out_shape=jax.ShapeDtypeStruct((8, LANES), f32),
        in_specs=[SMEM] + [VMEM] * 6,
        out_specs=VMEM,
        scratch_shapes=[
            pltpu.VMEM(wide.shape, f32),
            pltpu.VMEM(wide.shape, f32),
            pltpu.VMEM((ELEM, ELEM, LANES), f32),
            pltpu.VMEM((12 * count_y, LANES), f32),
        ],
        compiler_params=PARAMS,
    )(nodal_disp, *halos)
    loads = pl.pallas_call(
        gather_kernel,
        out_shape=jax.ShapeDtypeStruct(sizes + block.shape, f32),
        in_specs=[VMEM],
        out_specs=VMEM,
        scratch_shapes=[direct_sems, direct_sems],
        compiler_params=pltpu.CompilerParams(
            vmem_limit_bytes=48 * 2**20, collective_id=1, has_side_effects=True
        ),
    )(block)
    total_y = lax.axis_size("gy") * count_y
    fields = pltpu.VMEM((24, total_y, LANES), f32)
    nodes_out = jax.ShapeDtypeStruct(nodal_disp.shape, f32)
    return pl.pallas_call(
        functools.partial(cg_kernel, (count_x, count_y)),
        out_shape=(nodes_out, nodes_out),
        in_specs=[VMEM] * 2,
        out_specs=[VMEM] * 2,
        scratch_shapes=[
            pltpu.VMEM((groups * GROUP, total_y, LANES), f32),
            pltpu.VMEM((groups * per, total_y, LANES), f32),
            fields,
            fields,
            fields,
        ],
        compiler_params=PARAMS,
    )(gathered, loads)


def solution(mesh):
    in_specs = (P("gz", "gy", "gx"), P("gz", "gy", "gx"), P(None, "gz", "gy", "gx"))
    out_specs = (P(None, "gz", "gy", "gx"), P(None, "gz", "gy", "gx"))
    return jax.shard_map(
        per_device, mesh=mesh, in_specs=in_specs, out_specs=out_specs, check_vma=False
    )
```

```python
import functools

import jax
import jax.numpy as jnp
import numpy as np
from jax import lax
from jax.experimental import pallas as pl
from jax.experimental.pallas import tpu as pltpu
from jax.sharding import PartitionSpec as P

ELEM = 16
CGSTEPS = 8
QUANTUM = 64
DAMPING = 0.5
LANES = 128
SLOTS = LANES // ELEM
PAIRS = ((0, 0), (0, 1), (0, 2), (1, 1), (1, 2), (2, 2))
PAIR_OF = ((0, 1, 2), (1, 3, 4), (2, 4, 5))
GROUP = 12
GROUPS = 5
HALF = 8
CHUNKS = 3 * ELEM // HALF

POSITION = (np.arange(ELEM) + 0.5) / ELEM
LINEAR = np.stack([1.0 - POSITION, POSITION])
SQUARED = np.stack([LINEAR[0] * LINEAR[0], LINEAR[0] * LINEAR[1], LINEAR[1] * LINEAR[1]])


def lane_of(shape):
    return lax.broadcasted_iota(jnp.int32, shape, len(shape) - 1)


def pack_face(load, first):
    total = load(0)
    slot = lane_of(total.shape) // ELEM
    total = pltpu.roll(total, (-first) % LANES, 1) if first else total
    for group in range(1, HALF):
        piece = pltpu.roll(load(group), (ELEM * group - first) % LANES, 1)
        total = jnp.where(slot == group, piece, total)
    return total


def flip(index, step):
    return index + step - 2 * step * ((index // step) % 2)


class Gather:
    def __init__(self, ref, send_sem, recv_sem):
        self.ref, self.sems = ref, (send_sem, recv_sem)
        self.sizes = ref.shape[:3]
        size_x, size_y, size_z = self.sizes
        self.at = ix, iy, iz = tuple(lax.axis_index(axis) for axis in ("gx", "gy", "gz"))
        self.steps = []
        step = size_x // 2
        while step:
            self.steps.append(step)
            step //= 2
        self.z_peers = [{"gz": (iz + hop) % size_z} for hop in range(1, size_z)]
        self.y_peers = [{"gy": (iy + hop) % size_y} for hop in range(1, size_y)]
        self.x_peers = [{"gx": flip(ix, step)} for step in self.steps]
        self.peers = self.z_peers + self.y_peers + self.x_peers
        self.sent, self.phase, self.held = [], [], [ix]

    def send(self, source, arriving, peer):
        index = len(self.sent)

        def copy(ref):
            return pltpu.make_async_remote_copy(
                src_ref=ref,
                dst_ref=ref,
                send_sem=self.sems[0].at[index],
                recv_sem=self.sems[1].at[index],
                device_id=peer,
                device_id_type=MESH,
            )

        outgoing = copy(source)
        outgoing.start()
        self.sent.append(outgoing)
        self.phase.append(copy(arriving))

    def arrive(self):
        for copy in self.phase:
            copy.wait_recv()
        self.phase = []

    def start_z(self):
        (ix, iy, iz), size = self.at, self.sizes[2]
        for hop in range(1, size):
            other = (iz + size - hop) % size
            self.send(self.ref.at[ix, iy, iz], self.ref.at[ix, iy, other], self.z_peers[hop - 1])

    def start_y(self):
        (ix, iy, iz), size = self.at, self.sizes[1]
        for hop in range(1, size):
            other = (iy + size - hop) % size
            self.send(self.ref.at[ix, iy], self.ref.at[ix, other], self.y_peers[hop - 1])

    def start_x(self, number):
        step = self.steps[number]
        for own in self.held:
            self.send(self.ref.at[own], self.ref.at[flip(own, step)], self.x_peers[number])
        self.held = self.held + [flip(own, step) for own in self.held]

    def run_x(self):
        arrivals = [[] for _ in self.steps]

        def push(own, first):
            for number in range(first, len(self.steps)):
                other = flip(own, self.steps[number])
                self.send(self.ref.at[own], self.ref.at[other], self.x_peers[number])
                arrivals[number].append((self.phase.pop(), other))

        push(self.at[0], 0)
        for number in range(len(self.steps)):
            for copy, block in arrivals[number]:
                copy.wait_recv()
                push(block, number + 1)

    def finish(self):
        for copy in self.sent:
            copy.wait_send()


MESH = pl.DeviceIdType.MESH


def neighbour_barrier(sides, peers):
    barrier = pltpu.get_barrier_semaphore()
    count = len(peers)
    for peer in peers:
        pl.semaphore_signal(barrier, inc=1, device_id=peer, device_id_type=MESH)
    for axis, delta, exists in sides:

        @pl.when(exists)
        def _(axis=axis, delta=delta):
            pl.semaphore_signal(
                barrier, inc=1, device_id={axis: lax.axis_index(axis) + delta}, device_id_type=MESH
            )

        count = count + exists.astype(jnp.int32)
    pl.semaphore_wait(barrier, count)


def ramp(shape, axis):
    index = lax.broadcasted_iota(jnp.int32, shape, axis) % ELEM
    return (index.astype(jnp.float32) + 0.5) * (1.0 / ELEM)


def powers(position, squared):
    rest = 1.0 - position
    if squared:
        return (rest * rest, rest * position, position * position)
    return (rest, position)


def x_weights(group, squared):
    shape = (LANES, LANES)
    count_x = LANES // ELEM
    row, column = (lax.broadcasted_iota(jnp.int32, shape, axis) for axis in (0, 1))
    weights = powers(ramp(shape, 0), squared)
    total = jnp.zeros(shape, jnp.float32)
    for u, weight in enumerate(weights):
        slot = group * len(weights) + u
        mine = jnp.logical_and(column // count_x == slot, row // ELEM == column % count_x)
        total = jnp.where(mine, weight * (1.0 / ELEM**2), total)
    return total


def moments_row(ey, ref_ref, x_low_ref, x_high_ref, u_ref, count_y):
    by_y = powers(ramp((ELEM, LANES), 0), True)
    lane_8 = lane_of((8, LANES))
    sums = []
    for half in range(ELEM // 8):
        squares = [[None] * 3 for _ in PAIRS]
        at = ey * ELEM + 8 * half
        for z in range(ELEM):
            slopes = slopes_at(z, at, ref_ref, x_low_ref, x_high_ref, lane_8)
            for index, (c, d) in enumerate(PAIRS):
                product = slopes[c] * slopes[d]
                for level in range(3):
                    term = float(SQUARED[level, z]) * product
                    squares[index][level] = term if z == 0 else squares[index][level] + term
        sums.append(squares)
    for index in range(len(PAIRS)):
        for level in range(3):
            for t in range(3):
                total = sum(
                    sums[half][index][level] * by_y[t][8 * half : 8 * half + 8, :]
                    for half in range(2)
                )
                kind = index * 9 + level * 3 + t
                u_ref[pl.ds(kind * count_y + ey, 1), :] = jnp.sum(total, axis=0, keepdims=True)


def slopes_at(z, at, ref_ref, x_low_ref, x_high_ref, lane_8):
    group, part = z % HALF, z // HALF
    at = pl.multiple_of(at, 8)
    row = pl.multiple_of(at + 8, 8)
    here = ref_ref[z + 1, pl.ds(row, 8), :]
    left = jnp.where(
        lane_8 == 0,
        pltpu.roll(x_low_ref[part, pl.ds(at, 8), :], (2 * LANES - ELEM * group - ELEM + 1) % LANES, 1),
        pltpu.roll(here, 1, 1),
    )
    right = jnp.where(
        lane_8 == LANES - 1,
        pltpu.roll(x_high_ref[part, pl.ds(at, 8), :], (LANES - 1 - ELEM * group) % LANES, 1),
        pltpu.roll(here, LANES - 1, 1),
    )
    return (
        0.5 * (ref_ref[z + 2, pl.ds(row, 8), :] - ref_ref[z, pl.ds(row, 8), :]),
        0.5 * (ref_ref[z + 1, pl.ds(at + 9, 8), :] - ref_ref[z + 1, pl.ds(at + 7, 8), :]),
        0.5 * (right - left),
    )


def contract_x(u_ref, squared, rows):
    total = 0.0
    for group in range(u_ref.shape[0] // rows):
        total = total + jnp.dot(
            u_ref[group * rows : (group + 1) * rows, :],
            x_weights(group, squared),
            precision=lax.Precision.HIGHEST,
            preferred_element_type=jnp.float32,
        )
    return total


def halo_kernel(
    image_ref, deformed_ref,
    wide_ref, from_low_ref, from_high_ref, ref_ref, x_low_ref, x_high_ref, gathered_ref,
    to_low_ref, to_high_ref, ref_low_ref, ref_high_ref, u_ref,
    z_low_ref, z_high_ref, y_low_ref, y_high_ref, send_sem, recv_sem, gather_send, gather_recv,
):
    size_z, size_y, _ = image_ref.shape
    count_y = size_y // ELEM
    low, high = {}, {}
    for axis in ("gz", "gy", "gx"):
        low[axis] = lax.axis_index(axis) > 0
        high[axis] = lax.axis_index(axis) < lax.axis_size(axis) - 1
    sides = [(axis, -1, low[axis]) for axis in low] + [(axis, 1, high[axis]) for axis in high]
    gather = Gather(gathered_ref, gather_send, gather_recv)
    neighbour_barrier(sides, gather.peers)
    copies = []

    def send(axis, delta, source, target):
        index = len(copies)
        copy = pltpu.make_async_remote_copy(
            src_ref=source,
            dst_ref=target,
            send_sem=send_sem.at[index],
            recv_sem=recv_sem.at[index],
            device_id={axis: lax.axis_index(axis) + delta},
            device_id_type=MESH,
        )
        sends, receives = (high[axis], low[axis]) if delta > 0 else (low[axis], high[axis])
        copies.append((copy, sends))

        @pl.when(sends)
        def _():
            copy.start()

        def arrive():
            @pl.when(receives)
            def _():
                copy.wait_recv()

        def blank(*refs):
            @pl.when(jnp.logical_not(receives))
            def _():
                for ref in refs:
                    ref[...] = jnp.zeros(ref.shape, ref.dtype)

        arrive.blank = blank
        return arrive

    rows = pl.ds(ELEM, size_y)
    middle = pl.ds(ELEM, ELEM)
    first_rows, last_rows = pl.ds(0, ELEM), pl.ds(size_y - ELEM, ELEM)
    into_low, into_high = pl.ds(0, ELEM), pl.ds(ELEM + size_y, ELEM)
    others = [
        send("gz", 1, image_ref.at[size_z - 1], z_low_ref),
        send("gz", -1, image_ref.at[0], z_high_ref),
        send("gy", 1, image_ref.at[:, pl.ds(size_y - 8, 8)], y_low_ref),
        send("gy", -1, image_ref.at[:, pl.ds(0, 8)], y_high_ref),
    ]
    waits = []
    for half in range(ELEM // HALF):
        depth = pl.ds(half * HALF, HALF)
        waits.append(
            [
                send("gz", 1, deformed_ref.at[depth], wide_ref.at[depth, rows]),
                send("gz", -1, deformed_ref.at[depth], wide_ref.at[pl.ds(2 * ELEM + half * HALF, HALF), rows]),
            ]
        )
    center = [
        send("gy", 1, deformed_ref.at[:, last_rows], wide_ref.at[middle, into_low]),
        send("gy", -1, deformed_ref.at[:, first_rows], wide_ref.at[middle, into_high]),
    ]
    for first, face in ((0, ref_low_ref), (LANES - ELEM, ref_high_ref)):
        for half in range(ELEM // HALF):
            face[half] = pack_face(lambda z: image_ref[half * HALF + z], first)
    others += [
        send("gx", 1, ref_high_ref, x_low_ref),
        send("gx", -1, ref_low_ref, x_high_ref),
    ]
    for arrive, ref in zip(
        others, (z_low_ref, z_high_ref, y_low_ref, y_high_ref, x_low_ref, x_high_ref)
    ):
        arrive.blank(ref)
    waits[0][0].blank(wide_ref.at[pl.ds(0, ELEM), rows])
    waits[0][1].blank(wide_ref.at[pl.ds(2 * ELEM, ELEM), rows])
    wide_ref[middle, rows] = deformed_ref[...]
    ref_ref[1 : 1 + size_z, 8 : 8 + size_y] = image_ref[...]
    u_ref[...] = jnp.zeros_like(u_ref)

    final = []

    def x_faces(chunks, arrivals):
        start = pl.ds(chunks[0] * HALF, len(chunks) * HALF)
        arrivals[0].blank(wide_ref.at[start, into_low])
        arrivals[1].blank(wide_ref.at[start, into_high])
        for arrive in arrivals:
            arrive()
        for chunk in chunks:
            for first, face in ((0, to_low_ref), (LANES - ELEM, to_high_ref)):
                face[chunk] = pack_face(lambda z: wide_ref[chunk * HALF + z], first)
            pair = [
                send("gx", 1, to_high_ref.at[chunk], from_low_ref.at[chunk]),
                send("gx", -1, to_low_ref.at[chunk], from_high_ref.at[chunk]),
            ]
            pair[0].blank(from_low_ref.at[chunk])
            pair[1].blank(from_high_ref.at[chunk])
            final.extend(pair)

    def forward_y(half):
        result = []
        for side in range(2):
            waits[half][side]()
            chunk = side * 2 * (ELEM // HALF) + half
            depth = pl.ds(chunk * HALF, HALF)
            result.append(
                (
                    chunk,
                    [
                        send("gy", 1, wide_ref.at[depth, pl.ds(size_y, ELEM)], wide_ref.at[depth, into_low]),
                        send("gy", -1, wide_ref.at[depth, pl.ds(ELEM, ELEM)], wide_ref.at[depth, into_high]),
                    ],
                )
            )
        return result

    for arrive in others:
        arrive()
    ref_ref[0, 8 : 8 + size_y] = z_low_ref[...]
    ref_ref[size_z + 1, 8 : 8 + size_y] = z_high_ref[...]
    ref_ref[1 : 1 + size_z, 0:8] = y_low_ref[...]
    ref_ref[1 : 1 + size_z, 8 + size_y : 16 + size_y] = y_high_ref[...]

    def moments(ey, carry):
        moments_row(ey, ref_ref, x_low_ref, x_high_ref, u_ref, count_y)
        return carry

    lax.fori_loop(0, count_y // 2, moments, 0)
    x_faces((2, 3), center)
    early = forward_y(0)
    lax.fori_loop(count_y // 2, count_y, moments, 0)
    gathered_ref[gather.at[0], gather.at[1], gather.at[2]] = contract_x(
        u_ref, True, GROUP * count_y
    )
    gather.start_z()
    for chunk, arrivals in early:
        x_faces((chunk,), arrivals)
    late = forward_y(1)
    gather.arrive()
    gather.start_y()
    for chunk, arrivals in late:
        x_faces((chunk,), arrivals)
    gather.arrive()
    gather.run_x()
    for arrive in final:
        arrive()
    gather.finish()
    for copy, sends in copies:

        @pl.when(sends)
        def _(copy=copy):
            copy.wait_send()


HALO_COPIES = 4 + 2 * (ELEM // HALF) + 2 + 2 + 4 * (ELEM // HALF) + 2 * CHUNKS


def gather_kernel(block_ref, gathered_ref, send_sem, recv_sem):
    sizes = gathered_ref.shape[:3]
    at = tuple(lax.axis_index(axis) for axis in ("gx", "gy", "gz"))
    hops = [
        (x, y, z)
        for z in range(sizes[2])
        for y in range(sizes[1])
        for x in range(sizes[0])
        if x or y or z
    ]

    def away(hop, sign):
        return tuple((at[i] + sizes[i] + sign * hop[i]) % sizes[i] for i in range(3))

    targets = [away(hop, 1) for hop in hops]
    peers = [dict(zip(("gx", "gy", "gz"), target)) for target in targets]
    neighbour_barrier([], peers)
    outgoing = []
    for index, peer in enumerate(peers):
        copy = pltpu.make_async_remote_copy(
            src_ref=block_ref,
            dst_ref=gathered_ref.at[at],
            send_sem=send_sem.at[index],
            recv_sem=recv_sem.at[index],
            device_id=peer,
            device_id_type=MESH,
        )
        copy.start()
        outgoing.append(copy)
    gathered_ref[at] = block_ref[...]
    for index, hop in enumerate(hops):
        pltpu.make_async_remote_copy(
            src_ref=block_ref,
            dst_ref=gathered_ref.at[away(hop, -1)],
            send_sem=send_sem.at[index],
            recv_sem=recv_sem.at[index],
            device_id=peers[index],
            device_id_type=MESH,
        ).wait_recv()
    for copy in outgoing:
        copy.wait_send()


def element_kernel(
    nodes_ref, wide_ref, from_low_ref, from_high_ref, ref_ref, x_low_ref, x_high_ref,
    out_ref, low_ref, high_ref, warp_ref, u_ref,
):
    rows_wide = wide_ref.shape[1]
    size_y = rows_wide - 2 * ELEM
    count_y, count_x = size_y // ELEM, LANES // ELEM
    lane_wide = lane_of((rows_wide, LANES))

    def spread(chunk, carry):
        left, right = from_low_ref[chunk], from_high_ref[chunk]
        for group in range(HALF):
            z = chunk * HALF + group
            centre = wide_ref[z]
            low = pltpu.roll(left, (2 * LANES - ELEM - ELEM * group) % LANES, 1)
            low_ref[z] = jnp.where(lane_wide >= LANES - ELEM, low, centre)
            high = pltpu.roll(right, (LANES - ELEM * group) % LANES, 1)
            high_ref[z] = jnp.where(lane_wide < ELEM, high, centre)
        return carry

    lax.fori_loop(0, CHUNKS, spread, 0)
    by_y = powers(ramp((ELEM, LANES), 0), False)

    lane_16 = lane_of((ELEM, LANES))
    lane_8 = lane_of((8, LANES))

    def row(ey, carry):
        base = pl.multiple_of(ey * ELEM, ELEM)

        def element(source, ex):
            starts, shares = [], []
            for c in range(3):
                total = 0
                for offset in range(8):
                    total = total + nodes_ref[
                        c, offset >> 2, ey + (offset >> 1 & 1), ex + (offset & 1)
                    ]
                starts.append((total >> 9) + ELEM)
                shares.append((total & 511).astype(jnp.float32) * (1.0 / (8 * QUANTUM)))
            sz, sy, sx = starts
            fz, fy, fx = shares
            ys = base + sy
            back = (2 * LANES + ELEM - sx) % LANES
            back_next = (2 * LANES + ELEM - 1 - sx) % LANES
            mine = lane_16 // ELEM == ex

            def plane(z):
                return (1.0 - fy) * source[sz + z, pl.ds(ys, ELEM), :] + fy * source[
                    sz + z, pl.ds(ys + 1, ELEM), :
                ]

            before = plane(0)
            for z in range(ELEM):
                after = plane(z + 1)
                mixed = (1.0 - fz) * before + fz * after
                before = after
                value = (1.0 - fx) * pltpu.roll(mixed, back, 1) + fx * pltpu.roll(
                    mixed, back_next, 1
                )
                warp_ref[z] = jnp.where(mine, value, warp_ref[z])

        element(low_ref, 0)

        def middle(ex, carry):
            element(wide_ref, ex)
            return carry

        lax.fori_loop(1, count_x - 1, middle, 0)
        element(high_ref, count_x - 1)

        sums = []
        for half in range(ELEM // 8):
            loads = [[None] * 2 for _ in range(3)]
            at = base + 8 * half
            for z in range(ELEM):
                slopes = slopes_at(z, at, ref_ref, x_low_ref, x_high_ref, lane_8)
                here = ref_ref[z + 1, pl.ds(pl.multiple_of(at + 8, 8), 8), :]
                mismatch = here - warp_ref[z, 8 * half : 8 * half + 8, :]
                for c in range(3):
                    product = slopes[c] * mismatch
                    for a in range(2):
                        term = float(LINEAR[a, z]) * product
                        loads[c][a] = term if z == 0 else loads[c][a] + term
            sums.append(loads)
        for c in range(3):
            for a in range(2):
                for b in range(2):
                    total = sum(
                        sums[half][c][a] * by_y[b][8 * half : 8 * half + 8, :]
                        for half in range(2)
                    )
                    kind = c * 4 + a * 2 + b
                    u_ref[pl.ds(kind * count_y + ey, 1), :] = jnp.sum(total, axis=0, keepdims=True)
        return carry

    lax.fori_loop(0, count_y, row, 0)
    out_ref[...] = contract_x(u_ref, False, out_ref.shape[0])


def cg_kernel(axes, gathered_ref, loads_ref, update_ref, residual_ref, m_ref, b_ref, s_ref, r_ref, d_ref):
    count_x, count_y = axes
    groups_x, groups_y, groups_z = gathered_ref.shape[:3]
    places = groups_z * groups_x
    total_y = groups_y * count_y
    elems_x = lax.axis_size("gx") * count_x
    shape = (total_y, LANES)
    lane = lane_of(shape)
    line = lax.broadcasted_iota(jnp.int32, shape, 0)
    slot = lane // count_x
    per = 8 // count_y

    def unpack(source, target, lines, pair, carry):
        at = pl.multiple_of(pair * 8, 8)
        tiles = [
            [
                source[j % groups_x, iy, j // groups_x, pl.ds(at, 8), :]
                for iy in range(groups_y)
            ]
            for j in range(places)
        ]
        for half in range(per):
            values = [
                jnp.concatenate(
                    [tile[half * count_y : (half + 1) * count_y] for tile in tiles[j]], axis=0
                )
                for j in range(places)
            ]
            step = 1
            while step < places:
                bit = (slot // step) % 2 == 0
                fresh = list(values)
                for j in range(places):
                    if (j // step) % 2 == 0:
                        first, second = values[j], values[j + step]
                        fresh[j] = jnp.where(bit, first, pltpu.roll(second, step * count_x, 1))
                        fresh[j + step] = jnp.where(
                            bit, pltpu.roll(first, LANES - step * count_x, 1), second
                        )
                values = fresh
                step *= 2
            for high in range(places):
                target[high * lines + pair * per + half] = values[high]
        return carry

    lax.fori_loop(0, GROUP // per, functools.partial(unpack, gathered_ref, m_ref, GROUP), 0)
    unpack(loads_ref, b_ref, per, 0, 0)

    edge = {
        2: (lane % elems_x == 0, lane % elems_x == elems_x - 1, 1, 1),
        1: (line == 0, line == total_y - 1, 1, 0),
        0: (lane < elems_x, lane >= LANES - elems_x, elems_x, 1),
    }
    corner_list = [(a, b, g) for a in range(2) for b in range(2) for g in range(2)]
    keys = [(c,) + k for c in range(3) for k in corner_list]
    position = {key: index for index, key in enumerate(keys)}
    one = jnp.ones(shape, jnp.float32)
    own = {}
    for corner in corner_list:
        mask = one
        for dim in range(3):
            if corner[dim]:
                mask = jnp.where(edge[dim][1], mask, 0.0)
        own[corner] = mask

    def assemble(parts):
        for dim in range(3):
            first, last, shift, axis = edge[dim]
            extent = shape[axis]
            fresh = {}
            for key in keys:
                if key[1 + dim] == 0:
                    other = key[: 1 + dim] + (1,) + key[2 + dim :]
                    low, high = parts[key], parts[other]
                    fresh[key] = low + jnp.where(first, 0.0, pltpu.roll(high, shift, axis))
                    fresh[other] = high + jnp.where(last, 0.0, pltpu.roll(low, extent - shift, axis))
            parts = fresh
        return parts

    def squares(parts):
        total = {}
        for corner in corner_list:
            total[corner] = sum(parts[(c,) + corner] * parts[(c,) + corner] for c in range(3))
        return sum(total[corner] * own[corner] for corner in corner_list)

    parts = {}
    for c, a, b, g in keys:
        kind = c * 4 + a * 2 + b
        parts[c, a, b, g] = b_ref[((kind // per) * 2 + g) * per + kind % per]
    parts = assemble(parts)
    for key in keys:
        s_ref[position[key]] = jnp.zeros(shape, jnp.float32)
        r_ref[position[key]] = parts[key]
        d_ref[position[key]] = parts[key]

    def step(index, norm_now):
        d = {key: d_ref[position[key]] for key in keys}
        image = {key: None for key in keys}
        for p, (first, second) in enumerate(PAIRS):
            orders = ((first, second),) if first == second else ((first, second), (second, first))
            for s in range(3):
                for t in range(3):
                    for u in range(3):
                        kind = p * 9 + s * 3 + t
                        value = m_ref[((kind // GROUP) * 3 + u) * GROUP + kind % GROUP]
                        for c, e in orders:
                            for a, b, g in corner_list:
                                q = (s - a, t - b, u - g)
                                if min(q) < 0 or max(q) > 1:
                                    continue
                                term = value * d[(e,) + q]
                                key = (c, a, b, g)
                                image[key] = term if image[key] is None else image[key] + term
        dots = sum(image[key] * d[key] for key in keys) + DAMPING * squares(d)
        alpha = norm_now / jnp.sum(dots)
        image = assemble(image)
        residual = {}
        for key in keys:
            at = position[key]
            s_ref[at] = s_ref[at] + alpha * d[key]
            residual[key] = r_ref[at] - alpha * (image[key] + DAMPING * d[key])
            r_ref[at] = residual[key]
        norm_next = jnp.sum(squares(residual))
        beta = norm_next / norm_now
        for key in keys:
            d_ref[position[key]] = residual[key] + beta * d[key]
        return norm_next

    start = {key: r_ref[position[key]] for key in keys}
    lax.fori_loop(0, CGSTEPS, step, jnp.sum(squares(start)))

    place = lax.axis_index("gz") * lax.axis_size("gx") + lax.axis_index("gx")
    first_lane = place * count_x
    first_line = lax.axis_index("gy") * count_y
    last_lane = (first_lane + count_x) % LANES
    last_line = (first_line + count_y) % total_y
    for source, out, scale in ((s_ref, update_ref, float(QUANTUM)), (r_ref, residual_ref, 1.0)):
        for c in range(3):
            for a in range(2):
                merged = []
                for b in range(2):
                    merged.append(
                        jnp.where(
                            lane == last_lane,
                            pltpu.roll(source[position[c, a, b, 1]], 1, 1),
                            source[position[c, a, b, 0]],
                        )
                    )
                value = jnp.where(line == last_line, pltpu.roll(merged[1], 1, 0), merged[0])
                value = pltpu.roll(value, (LANES - first_lane) % LANES, 1)
                value = pltpu.roll(value, (total_y - first_line) % total_y, 0)
                out[c, a] = scale * value[: count_y + 1, : count_x + 1]


VMEM = pl.BlockSpec(memory_space=pltpu.VMEM)
SMEM = pl.BlockSpec(memory_space=pltpu.SMEM)
PARAMS = pltpu.CompilerParams(vmem_limit_bytes=48 * 2**20)


def per_device(ref_image, deformed_image, nodal_disp):
    size_z, size_y, size_x = ref_image.shape
    count_y, count_x = size_y // ELEM, size_x // ELEM
    f32 = jnp.float32
    per = 8 // count_y
    sizes = tuple(lax.axis_size(axis) for axis in ("gx", "gy", "gz"))
    groups = sizes[0] * sizes[2]
    gather_sems = pltpu.SemaphoreType.DMA((sum(sizes) - 3,))
    direct_sems = pltpu.SemaphoreType.DMA((groups * sizes[1] - 1,))
    moments = jax.ShapeDtypeStruct(sizes + (GROUP * count_y, LANES), f32)
    wide = jax.ShapeDtypeStruct((3 * ELEM, size_y + 2 * ELEM, LANES), f32)
    face = jax.ShapeDtypeStruct((CHUNKS, size_y + 2 * ELEM, LANES), f32)
    ref_face = jax.ShapeDtypeStruct((ELEM // HALF, size_y, LANES), f32)
    padded = jax.ShapeDtypeStruct((size_z + 2, size_y + 16, LANES), f32)
    plane = pltpu.VMEM((size_y, LANES), f32)
    edge = pltpu.VMEM((size_z, 8, LANES), f32)
    *halos, gathered = pl.pallas_call(
        halo_kernel,
        out_shape=(wide, face, face, padded, ref_face, ref_face, moments),
        in_specs=[VMEM] * 2,
        out_specs=[VMEM] * 7,
        scratch_shapes=[
            pltpu.VMEM(face.shape, f32),
            pltpu.VMEM(face.shape, f32),
            pltpu.VMEM(ref_face.shape, f32),
            pltpu.VMEM(ref_face.shape, f32),
            pltpu.VMEM((GROUP * GROUPS * count_y, LANES), f32),
            plane,
            plane,
            edge,
            edge,
            pltpu.SemaphoreType.DMA((HALO_COPIES,)),
            pltpu.SemaphoreType.DMA((HALO_COPIES,)),
            gather_sems,
            gather_sems,
        ],
        compiler_params=pltpu.CompilerParams(
            vmem_limit_bytes=48 * 2**20, collective_id=0, has_side_effects=True
        ),
    )(ref_image, deformed_image)
    block = pl.pallas_call(
        element_kernel,
        out_shape=jax.ShapeDtypeStruct((8, LANES), f32),
        in_specs=[SMEM] + [VMEM] * 6,
        out_specs=VMEM,
        scratch_shapes=[
            pltpu.VMEM(wide.shape, f32),
            pltpu.VMEM(wide.shape, f32),
            pltpu.VMEM((ELEM, ELEM, LANES), f32),
            pltpu.VMEM((12 * count_y, LANES), f32),
        ],
        compiler_params=PARAMS,
    )(nodal_disp, *halos)
    loads = pl.pallas_call(
        gather_kernel,
        out_shape=jax.ShapeDtypeStruct(sizes + block.shape, f32),
        in_specs=[VMEM],
        out_specs=VMEM,
        scratch_shapes=[direct_sems, direct_sems],
        compiler_params=pltpu.CompilerParams(
            vmem_limit_bytes=48 * 2**20, collective_id=1, has_side_effects=True
        ),
    )(block)
    total_y = lax.axis_size("gy") * count_y
    fields = pltpu.VMEM((24, total_y, LANES), f32)
    nodes_out = jax.ShapeDtypeStruct(nodal_disp.shape, f32)
    return pl.pallas_call(
        functools.partial(cg_kernel, (count_x, count_y)),
        out_shape=(nodes_out, nodes_out),
        in_specs=[VMEM] * 2,
        out_specs=[VMEM] * 2,
        scratch_shapes=[
            pltpu.VMEM((groups * GROUP, total_y, LANES), f32),
            pltpu.VMEM((groups * per, total_y, LANES), f32),
            fields,
            fields,
            fields,
        ],
        compiler_params=PARAMS,
    )(gathered, loads)


def solution(mesh):
    in_specs = (P("gz", "gy", "gx"), P("gz", "gy", "gx"), P(None, "gz", "gy", "gx"))
    out_specs = (P(None, "gz", "gy", "gx"), P(None, "gz", "gy", "gx"))
    return jax.shard_map(
        per_device, mesh=mesh, in_specs=in_specs, out_specs=out_specs, check_vma=False
    )
```
